512 devices in a mesh: dp: 64 (over z, y), ctx: 8 (over x, core).
Axes of the slice: x: 4, y: 8, z: 8, core: 2. Of those that a mesh axis runs over, the one named last changes fastest.
Arguments:
- queries: bfloat16 [65536, 4096], P(('dp', 'ctx')), may hold values from -6 to 6
- key_rows: bfloat16 [65536, 512], P(('dp', 'ctx')), may hold values from -6 to 6
- value_rows: bfloat16 [65536, 512], P(('dp', 'ctx')), may hold values from -6 to 6
- out_grad: bfloat16 [65536, 4096], P(('dp', 'ctx')), may hold values from -6 to 6
- doc_lengths: int32 [128, 8], P('dp'), may hold values from 1 to 256, 512 in all within a row
- served_positions: int32 [64, 8, 64, 2], P('dp', 'ctx'), may hold values from 0 to 511, as said below
Outputs:
- attended: bfloat16 [65536, 4096], P(('dp', 'ctx'))
- log_sum_exp: float32 [65536, 32], P(('dp', 'ctx'))
- query_grad: bfloat16 [65536, 4096], P(('dp', 'ctx'))
The draws below stay inside these ranges and needn't reach their ends.
Inputs may be any that keep to these rules, and one draw needn't show every extreme that they name: For each j and s, the entries served_positions[j, c, i, s * 1 + t] over all c, i and t hold every position 0 to 511 exactly once. `doc_lengths`: each row sums to 512.
All inputs are finite; a program needn't handle non-finite values.
Results may differ from the reference program's by a relative error of at most 0.033.
Values may be sent and summed in bfloat16 or wider, within the bound.
A program may use at most 128 MiB of HBM per device.

```python
import math
import jax
import jax.numpy as jnp
import numpy as np
from jax import lax

HEAD_DIM = 128
HEADS = 32
KV_HEADS = 4
SUBS = 2
ROWS_PEER = 2
DOCS = 8
TOK_DEV = 128
SEQ_LEN = 512
ALL_ROWS = 65536
DOC_MOST = 256
N_DP = 64
N_CTX = 8


def draw_queries(key, part):
    key = jax.random.fold_in(key, 11)
    noise_key = jax.random.fold_in(key, 0)
    values_drawn = jnp.clip(jax.random.normal(noise_key, (ALL_ROWS, HEADS, HEAD_DIM)), -6.0, 6.0)
    return values_drawn.reshape(ALL_ROWS, HEADS * HEAD_DIM).astype(jnp.bfloat16)


def draw_key_rows(key, part):
    key = jax.random.fold_in(key, 12)
    noise_key = jax.random.fold_in(key, 0)
    values_drawn = jnp.clip(jax.random.normal(noise_key, (ALL_ROWS, KV_HEADS, HEAD_DIM)), -6.0, 6.0)
    return values_drawn.reshape(ALL_ROWS, KV_HEADS * HEAD_DIM).astype(jnp.bfloat16)


def draw_served_positions(key, part):
    key = jax.random.fold_in(key, 13)
    seq_keys = jax.random.split(key, N_DP * SUBS)
    orders = jax.vmap(lambda single: jax.random.permutation(single, SEQ_LEN))(seq_keys)
    orders = orders.reshape(N_DP, SUBS, N_CTX, N_DP, ROWS_PEER // SUBS).transpose(0, 2, 3, 1, 4)
    return orders.reshape(N_DP, N_CTX, N_DP, ROWS_PEER).astype(jnp.int32)


def steps_of(own_key, extent, pieces, low, high):
    def one(position, shards_of):
        draws = jax.random.uniform(jax.random.fold_in(jax.random.fold_in(own_key, 6), position), (shards_of,), jnp.float32, low / len(pieces), high / len(pieces))
        return jnp.repeat(jnp.exp(draws), extent[position] // shards_of).reshape((-1,) + (1,) * (len(extent) - position - 1))

    level = one(*pieces[0])
    for cut in pieces[1:]:
        level = level * one(*cut)
    return level


def split_up(amount, total, reach, slope):
    weights = [(1 << 20) // math.isqrt(rank ** slope) + 1 for rank in range(2, amount + 1)]
    spare, counts = total - reach - (amount - 1), [1] * (amount - 1)
    while spare > 0:
        movable = [i for i in range(amount - 1) if counts[i] < reach]
        mass, remaining = sum([weights[i] for i in movable]), spare
        for i in movable:
            extra = min(reach - counts[i], max(1, remaining * weights[i] // mass), spare)
            counts[i] = counts[i] + extra
            spare = spare - extra
    return np.array([reach] + counts)


def ragged_sizes(stream_key, number_of, total, reach, lean):
    if number_of == 2:
        one = jax.random.randint(stream_key, (), max(1, total - reach), min(reach, total - 1) + 1)
        return jnp.stack([one, total - one])
    sizes = jnp.asarray(split_up(number_of, total, reach, lean), jnp.int32)
    twos = (number_of - 1) // 2
    giver, sink = sizes[1:1 + 2 * twos:2], sizes[2:2 + 2 * twos:2]
    slack = jnp.minimum(giver - 1, reach - sink)
    moved = jax.random.randint(jax.random.fold_in(stream_key, 1), (twos,), 0, 1 << 20) % (slack + 1)
    sizes = sizes.at[1:1 + 2 * twos:2].set(giver - moved).at[2:2 + 2 * twos:2].set(sink + moved)
    return sizes[jax.random.permutation(jax.random.fold_in(stream_key, 2), number_of)]


def gaussian(own_key, dims, deviation, reach, cuts=(), held_as=jnp.bfloat16):
    gain = steps_of(own_key, dims, cuts, -0.22, 0.18) if cuts else 1.0
    result = jax.random.normal(own_key, dims, jnp.float32) * deviation * gain
    return jnp.minimum(jnp.maximum(result, -reach), reach).astype(held_as)


def setup_inputs(seed: int = 0) -> dict:
    key_list = jax.random.split(jax.random.key(seed), 7)
    return {
        "queries": draw_queries(jax.random.fold_in(key_list[6], 71), 0),
        "key_rows": draw_key_rows(jax.random.fold_in(key_list[6], 71), 0),
        "value_rows": gaussian(key_list[2], (ALL_ROWS, KV_HEADS * HEAD_DIM), 1.0, 6.0, ((0, 512),)),
        "out_grad": gaussian(key_list[3], (ALL_ROWS, HEADS * HEAD_DIM), 1.0, 6.0, ((0, 512),)),
        "doc_lengths": jax.vmap(lambda own: ragged_sizes(own, DOCS, SEQ_LEN, DOC_MOST, 2))(jax.random.split(key_list[4], (N_DP * SUBS))).reshape((N_DP * SUBS, DOCS)).astype(jnp.int32),
        "served_positions": draw_served_positions(jax.random.fold_in(key_list[6], 71), 0),
    }


NEG_FILL = -1e+30

def doc_index(positions, doc_ends):
    return lax.optimization_barrier(jnp.sum((positions[:, None] >= doc_ends[None, :]).astype(jnp.int32), axis=1))

def to_sequences(rows, width):
    each_sub = ROWS_PEER // SUBS
    shaped = rows.reshape(N_DP, N_CTX, N_DP, SUBS, each_sub, width)
    return shaped.transpose(2, 3, 1, 0, 4, 5).reshape(N_DP * SUBS, SEQ_LEN, width)

def to_rows(stacked, width):
    each_sub = ROWS_PEER // SUBS
    shaped = stacked.reshape(N_DP, SUBS, N_CTX, N_DP, each_sub, width)
    return shaped.transpose(3, 2, 0, 1, 4, 5).reshape(ALL_ROWS, width)

def one_sequence(packed):
    query_seq, grad_seq, query_pos, key_seq, value_seq, lengths = packed
    doc_ends = jnp.cumsum(lengths)
    key_pos = jnp.arange(SEQ_LEN, dtype=jnp.int32)
    visible = (key_pos[None, :] <= query_pos[:, None]) & (doc_index(key_pos, doc_ends)[None, :] == doc_index(query_pos, doc_ends)[:, None])
    group_size = HEADS // KV_HEADS
    score_scale = 1.0 / math.sqrt(HEAD_DIM)
    query_heads = query_seq.reshape(SEQ_LEN, HEADS, HEAD_DIM).astype(jnp.float32)
    grad_heads = grad_seq.reshape(SEQ_LEN, HEADS, HEAD_DIM).astype(jnp.float32)
    out_list, lse_list, grad_list = ([], [], [])
    for head_idx in range(KV_HEADS):
        key_head = key_seq[:, head_idx * HEAD_DIM:(head_idx + 1) * HEAD_DIM].astype(jnp.float32)
        value_head = value_seq[:, head_idx * HEAD_DIM:(head_idx + 1) * HEAD_DIM].astype(jnp.float32)
        query_group = query_heads[:, head_idx * group_size:(head_idx + 1) * group_size]
        grad_group = grad_heads[:, head_idx * group_size:(head_idx + 1) * group_size]
        scores = score_scale * jnp.einsum('nhd,kd->hnk', query_group, key_head)
        masked = jnp.where(visible[None], scores, NEG_FILL)
        row_max = lax.optimization_barrier(jnp.max(masked, axis=-1))
        row_sum = lax.optimization_barrier(jnp.sum(jnp.where(visible[None], jnp.exp(masked - row_max[..., None]), 0.0), axis=-1))
        lse_group = row_max + jnp.log(row_sum)
        weights = jnp.where(visible[None], jnp.exp(masked - lse_group[..., None]), 0.0)
        rounded = lax.optimization_barrier(weights.astype(jnp.bfloat16)).astype(jnp.float32)
        out_group = jnp.einsum('hnk,kd->nhd', rounded, value_head).astype(jnp.bfloat16)
        delta_rows = lax.optimization_barrier(jnp.sum(grad_group * out_group.astype(jnp.float32), axis=-1))
        prob_grad = jnp.einsum('nhd,kd->hnk', grad_group, value_head)
        score_grad = weights * (prob_grad - delta_rows.T[..., None])
        score_grad = lax.optimization_barrier(score_grad.astype(jnp.bfloat16)).astype(jnp.float32)
        query_part = (score_scale * jnp.einsum('hnk,kd->nhd', score_grad, key_head)).astype(jnp.bfloat16)
        out_list.append(out_group)
        lse_list.append(lse_group.T)
        grad_list.append(query_part)
    attended = jnp.concatenate(out_list, axis=1).reshape(SEQ_LEN, HEADS * HEAD_DIM)
    lse_all = jnp.concatenate(lse_list, axis=1)
    query_grad = jnp.concatenate(grad_list, axis=1).reshape(SEQ_LEN, HEADS * HEAD_DIM)
    return (attended, lse_all, query_grad)

def reference(queries, key_rows, value_rows, out_grad, doc_lengths, served_positions):
    feature = HEADS * HEAD_DIM
    kv_width = KV_HEADS * HEAD_DIM
    key_half = TOK_DEV // SUBS
    query_seqs = to_sequences(queries, feature)
    grad_seqs = to_sequences(out_grad, feature)
    pos_seqs = served_positions.reshape(N_DP, N_CTX, N_DP, SUBS, ROWS_PEER // SUBS)
    pos_seqs = pos_seqs.transpose(0, 3, 1, 2, 4).reshape(N_DP * SUBS, SEQ_LEN)
    key_seqs = key_rows.reshape(N_DP, N_CTX, SUBS, key_half, kv_width)
    key_seqs = key_seqs.transpose(0, 2, 1, 3, 4).reshape(N_DP * SUBS, SEQ_LEN, kv_width)
    value_seqs = value_rows.reshape(N_DP, N_CTX, SUBS, key_half, kv_width)
    value_seqs = value_seqs.transpose(0, 2, 1, 3, 4).reshape(N_DP * SUBS, SEQ_LEN, kv_width)
    attended, lse_all, query_grad = lax.map(one_sequence, (query_seqs, grad_seqs, pos_seqs, key_seqs, value_seqs, doc_lengths))
    return (to_rows(attended, feature), to_rows(lse_all, HEADS), to_rows(query_grad, feature))
```

```python
import functools
import math

import jax
import jax.numpy as jnp
from jax import lax
from jax.experimental import pallas as pl
from jax.experimental.pallas import tpu as pltpu
from jax.sharding import PartitionSpec as P

HEAD_DIM = 128
HEADS = 32
KV_HEADS = 4
GROUP = HEADS // KV_HEADS
SUBS = 2
NZ = 8
NY = 8
NX = 4
NCTX = 8
SLOTS = 32
HALF = 64
SEQ = 512
KV_ROWS = 272
NEG_FILL = -1e30
MESH = pl.DeviceIdType.MESH


def z_step(e, core):
    return e - 1 - 4 * core * (e // 3)


def kernel(rows, keys, values, info, out, lse_out, kv, got, res, lse,
           row_send, row_recv, kva_send, kvb_send, kv_recv, ring_send, ring_recv,
           res_send, res_recv, lse_send, lse_recv):
    dp = lax.axis_index("dp")
    ctx = lax.axis_index("ctx")
    z, y = dp // NY, dp % NY
    x, core = ctx // 2, ctx % 2
    right = z * NY + (y + 1) % NY
    left = z * NY + (y + NY - 1) % NY

    barrier = pltpu.get_barrier_semaphore()

    def greet(n, carry):
        other_z, other_ctx = n // NCTX, n % NCTX

        @pl.when(jnp.logical_or(other_z != z, other_ctx != ctx))
        def _():
            pl.semaphore_signal(barrier, inc=1, device_id=(other_z * NY + y, other_ctx),
                                device_id_type=MESH)

        return carry

    lax.fori_loop(0, NZ * NCTX, greet, 0)
    pl.semaphore_signal(barrier, inc=1, device_id=(left, ctx), device_id_type=MESH)
    pl.semaphore_signal(barrier, inc=1, device_id=(right, ctx), device_id_type=MESH)
    pl.semaphore_wait(barrier, NZ * NCTX + 1)

    def remote(src, dst, send, recv, dev):
        return pltpu.make_async_remote_copy(src_ref=src, dst_ref=dst, send_sem=send, recv_sem=recv,
                                            device_id=dev, device_id_type=MESH)

    def kv_parts(head, copy):
        cols = pl.ds(head * HEAD_DIM, HEAD_DIM)
        return ((keys.at[:, cols], kv.at[y, ctx, pl.ds(0, 128)]),
                (values.at[:, cols], kv.at[y, ctx, pl.ds(128, 128)]),
                (info.at[copy], kv.at[y, ctx, pl.ds(256, 16)]))

    far = ((z + 4) % NZ) * NY + y
    for head in range(KV_HEADS):
        is_self = jnp.logical_and(core == 0, x == head)

        @pl.when(is_self)
        def _(head=head):
            for src, dst in kv_parts(head, 0):
                pltpu.make_async_copy(src, dst, kv_recv).start()

        @pl.when(jnp.logical_not(is_self))
        def _(head=head):
            for src, dst in kv_parts(head, 0):
                remote(src, dst, kva_send, kv_recv, (dp, head * 2)).start()

        for src, dst in kv_parts(head, 1):
            remote(src, dst, kvb_send, kv_recv, (far, head * 2 + 1)).start()

    def send_rows(n, carry):
        copy, e, head = n % 2, (n // 2) % 4, n // 8
        server_z = (z - z_step(e, core) + 2 * NZ) % NZ
        home = (server_z + 4 * copy) % NZ
        src = rows.at[head * NZ + home]
        dst = got.at[(e % 2) * 16 + ctx * 2 + e // 2]
        is_self = jnp.logical_and(server_z == z, head * 2 + copy == ctx)

        @pl.when(is_self)
        def _():
            pltpu.make_async_copy(src, dst, row_recv).start()

        @pl.when(jnp.logical_not(is_self))
        def _():
            remote(src, dst, row_send, row_recv, (server_z * NY + y, head * 2 + copy)).start()

        return carry

    lax.fori_loop(0, SLOTS, send_rows, 0)

    def wait_bytes(ref, sem):
        pltpu.make_async_copy(ref, ref, sem).wait()

    def ring(step):
        from_left = kv.at[(y - step + NY) % NY]
        from_right = kv.at[(y + step) % NY]
        if step == 3:
            from_left = from_left.at[pl.ds(0, 4)]
            from_right = from_right.at[pl.ds(4, 4)]
        return (remote(from_left, from_left, ring_send.at[0, step], ring_recv.at[0, step], (right, ctx)),
                remote(from_right, from_right, ring_send.at[1, step], ring_recv.at[1, step], (left, ctx)))

    def ring_arrived(step):
        from_left = kv.at[(y - step - 1 + NY) % NY]
        from_right = kv.at[(y + step + 1) % NY]
        if step == 3:
            from_left = from_left.at[pl.ds(0, 4)]
            from_right = from_right.at[pl.ds(4, 4)]
        wait_bytes(from_left, ring_recv.at[0, step])
        wait_bytes(from_right, ring_recv.at[1, step])

    wait_bytes(kv.at[y], kv_recv)
    for copy in ring(0):
        copy.start()
    ring_arrived(0)
    for copy in ring(1):
        copy.start()
    ring_arrived(1)
    for copy in ring(2):
        copy.start()
    wait_bytes(got, row_recv)

    scale = 1.0 / math.sqrt(HEAD_DIM)
    to_log2 = scale * math.log2(math.e)
    lane = lax.broadcasted_iota(jnp.int32, (128, 128), 0)
    key_pos = lax.broadcasted_iota(jnp.int32, (256, SEQ), 1).astype(jnp.float32)
    lse_lane = lax.broadcasted_iota(jnp.int32, (256, 128), 1)
    server_home = (z + 4 * core) % NZ

    def pick(base):
        return jnp.where(lane == base, 16.0, jnp.where(lane == base + 1, 1.0, 0.0)).astype(jnp.bfloat16)

    def dot(a, b, dims):
        return lax.dot_general(a, b, (dims, ((), ())), preferred_element_type=jnp.float32)

    def one_sequence(y0, s):
        t = y0 * SUBS + s
        q = got[:, 0, t].reshape(256, HEAD_DIM)
        g = got[:, 1, t].reshape(256, HEAD_DIM)
        k = kv[y0, :, pl.ds(pl.multiple_of(s * HALF, HALF), HALF), :].reshape(SEQ, HEAD_DIM)
        v = kv[y0, :, pl.ds(pl.multiple_of(128 + s * HALF, HALF), HALF), :].reshape(SEQ, HEAD_DIM)
        marks = kv[y0, :, pl.ds(256, 16), :].reshape(128, 128)
        bounds = []
        for which in range(2):
            halves = [dot(marks, pick(e_lo * 64 + s * 32 + y * 4 + which * 2), ((1,), (0,)))
                      for e_lo in range(2)]
            whole = jnp.concatenate(halves, axis=0)
            bounds.append(jnp.concatenate([whole] * 4, axis=1))
        visible = jnp.logical_and(key_pos <= bounds[0], key_pos >= bounds[1])
        scores = jnp.where(visible, dot(q, k, ((1,), (1,))) * to_log2, NEG_FILL)
        top = jnp.max(scores, axis=1, keepdims=True)
        p = jnp.exp2(scores - top)
        total = jnp.sum(p, axis=1, keepdims=True)
        inverse = 1.0 / total
        att = (dot(p.astype(jnp.bfloat16), v, ((1,), (0,))) * inverse).astype(jnp.bfloat16)
        delta = jnp.sum(g.astype(jnp.float32) * att.astype(jnp.float32), axis=1, keepdims=True)
        grad = dot(g, v, ((1,), (1,)))
        ds = (p * (grad - delta)).astype(jnp.bfloat16)
        dq = (dot(ds, k, ((1,), (0,))) * (inverse * scale)).astype(jnp.bfloat16)
        res[:, y0, 0, s] = att.reshape(SLOTS, GROUP, HEAD_DIM)
        res[:, y0, 1, s] = dq.reshape(SLOTS, GROUP, HEAD_DIM)
        line = (top + jnp.log2(total)) * math.log(2.0)
        lse[...] = jnp.where(lse_lane == t, line, lse[...].reshape(256, 128)).reshape(SLOTS, GROUP, 128)

    def home_of(slot):
        e, c = (slot % 2) * 2 + slot // 16, (slot // 2) % NCTX
        home_z = (z + z_step(e, c % 2) + NZ) % NZ
        is_self = jnp.logical_and(home_z == z, c == ctx)
        return is_self, (home_z * NY + y, c)

    def serve(n, carry):
        y0 = (y + ((n + 1) // 2) * (2 * (n % 2) - 1) + NY) % NY

        def sub(s, inner):
            one_sequence(y0, s)
            return inner

        lax.fori_loop(0, SUBS, sub, 0)

        def give(slot, inner):
            is_self, dev = home_of(slot)
            src = res.at[slot, y0]
            dst = out.at[x, server_home, y0]

            @pl.when(is_self)
            def _():
                pltpu.make_async_copy(src, dst, res_recv).start()

            @pl.when(jnp.logical_not(is_self))
            def _():
                remote(src, dst, res_send, res_recv, dev).start()

            return inner

        lax.fori_loop(0, SLOTS, give, 0)
        return carry

    lse[...] = jnp.zeros_like(lse)
    lax.fori_loop(0, 3, serve, 0)
    ring_arrived(2)
    for copy in ring(3):
        copy.start()
    lax.fori_loop(3, 7, serve, 0)
    ring_arrived(3)
    lax.fori_loop(7, 8, serve, 0)

    def give_lse(slot, carry):
        is_self, dev = home_of(slot)
        src = lse.at[slot]
        dst = lse_out.at[x, server_home]

        @pl.when(is_self)
        def _():
            pltpu.make_async_copy(src, dst, lse_recv).start()

        @pl.when(jnp.logical_not(is_self))
        def _():
            remote(src, dst, lse_send, lse_recv, dev).start()

        return carry

    lax.fori_loop(0, SLOTS, give_lse, 0)

    wait_bytes(rows.at[pl.ds(0, SLOTS - 1)], row_send)
    wait_bytes(kv.at[0, pl.ds(0, 4)], kvb_send)

    @pl.when(core == 0)
    def _():
        wait_bytes(kv.at[0, pl.ds(0, 3)], kva_send)

    @pl.when(core != 0)
    def _():
        wait_bytes(kv.at[0, pl.ds(0, 4)], kva_send)

    for step in range(4):
        for copy in ring(step):
            copy.wait_send()
    wait_bytes(res.at[pl.ds(0, SLOTS - 1)], res_send)
    wait_bytes(lse.at[pl.ds(0, SLOTS - 1)], lse_send)
    wait_bytes(out, res_recv)
    wait_bytes(lse_out, lse_recv)


def local(queries, key_rows, value_rows, out_grad, doc_lengths, served_positions):
    dp = lax.axis_index("dp")
    core = lax.axis_index("ctx") % 2
    z = dp // NY

    def by_home(array):
        return array.reshape(NZ, 16, KV_HEADS, GROUP, HEAD_DIM).transpose(2, 0, 1, 3, 4)

    rows = jnp.stack([by_home(queries), by_home(out_grad)], axis=2)
    rows = rows.reshape(SLOTS, 2, 16, GROUP, HEAD_DIM)

    ends = jnp.cumsum(doc_lengths, axis=1)
    pos = served_positions.reshape(NZ, NY, SUBS)
    first = jnp.max(jnp.where(ends[None, None] <= pos[..., None], ends[None, None], 0), axis=-1)
    parts = jnp.stack([pos // 16, pos % 16, first // 16, first % 16], axis=-1)
    parts = parts.transpose(0, 2, 1, 3).reshape(NZ, HALF).astype(jnp.float32)
    slot = jnp.arange(8, dtype=jnp.int32)
    e = slot % 4
    home_z = (z + 4 * (slot // 4) + z_step(e, core) + NZ) % NZ
    chosen = home_z[:, None] == jnp.arange(NZ, dtype=jnp.int32)[None, :]
    marks = jnp.sum(jnp.where(chosen[:, :, None], parts[None], 0.0), axis=1)
    marks = marks.reshape(2, 2, 1, 128)
    info = jnp.broadcast_to(marks, (2, 2, GROUP, 128)).reshape(2, 16, 128).astype(jnp.bfloat16)

    bf16 = jnp.bfloat16
    dma = pltpu.SemaphoreType.DMA
    out, lse = pl.pallas_call(
        kernel,
        out_shape=(
            jax.ShapeDtypeStruct((KV_HEADS, NZ, NY, 2, SUBS, GROUP, HEAD_DIM), bf16),
            jax.ShapeDtypeStruct((KV_HEADS, NZ, GROUP, 128), jnp.float32),
        ),
        in_specs=[pl.BlockSpec(memory_space=pl.ANY)] * 4,
        out_specs=(pl.BlockSpec(memory_space=pl.ANY),) * 2,
        scratch_shapes=[
            pltpu.VMEM((NY, NCTX, KV_ROWS, HEAD_DIM), bf16),
            pltpu.VMEM((SLOTS, 2, 16, GROUP, HEAD_DIM), bf16),
            pltpu.VMEM((SLOTS, NY, 2, SUBS, GROUP, HEAD_DIM), bf16),
            pltpu.VMEM((SLOTS, GROUP, 128), jnp.float32),
            dma, dma, dma, dma, dma, dma((2, 4)), dma((2, 4)), dma, dma, dma, dma,
        ],
        compiler_params=pltpu.CompilerParams(
            collective_id=0, has_side_effects=True, vmem_limit_bytes=48 * 1024 * 1024
        ),
        cost_estimate=pl.CostEstimate(flops=4 * 10**9, bytes_accessed=8 * 2**20,
                                      transcendentals=2 * 2**20),
    )(rows, key_rows, value_rows, info)

    def to_rows(array):
        return array.transpose(1, 2, 3, 0, 4, 5).reshape(128, HEADS * HEAD_DIM)

    lse_rows = lse[..., :16].transpose(1, 3, 0, 2).reshape(128, HEADS)
    return to_rows(out[:, :, :, 0]), lse_rows, to_rows(out[:, :, :, 1])


def solution(mesh):
    in_specs = (
        P(("dp", "ctx"), None),
        P(("dp", "ctx"), None),
        P(("dp", "ctx"), None),
        P(("dp", "ctx"), None),
        P("dp", None),
        P("dp", "ctx", None, None),
    )
    out_specs = (P(("dp", "ctx"), None), P(("dp", "ctx"), None), P(("dp", "ctx"), None))
    return jax.shard_map(local, mesh=mesh, in_specs=in_specs, out_specs=out_specs, check_vma=False)
```

```python
import functools
import math

import jax
import jax.numpy as jnp
from jax import lax
from jax.experimental import pallas as pl
from jax.experimental.pallas import tpu as pltpu
from jax.sharding import PartitionSpec as P

HEAD_DIM = 128
HEADS = 32
KV_HEADS = 4
GROUP = HEADS // KV_HEADS
SUBS = 2
NZ = 8
NY = 8
NX = 4
NCTX = 8
SLOTS = 32
HALF = 64
SEQ = 512
PLACES = NY
TILES = 4 * PLACES + 1
EARLY = 3
KV_ROWS = 272
NEG_FILL = -1e30
MESH = pl.DeviceIdType.MESH


def z_step(e, core):
    return e - 1 - 4 * core * (e // 3)


def rank(distance):
    return jnp.where(distance <= 4, jnp.maximum(2 * distance - 1, 0), 16 - 2 * distance)


def kernel(queries, grads, keys, values, lengths, positions, out,
           rows, kv_out, kv, got, res, lse, second,
           row_send, row_recv, kva_send, kvb_send, kv_recv, ring_send, ring_recv,
           res_send, res_recv):
    dp = lax.axis_index("dp")
    ctx = lax.axis_index("ctx")
    z, y = lax.div(dp, NY), lax.rem(dp, NY)
    x, core = lax.div(ctx, 2), lax.rem(ctx, 2)
    right = z * NY + lax.rem(y + 1, NY)
    left = z * NY + lax.rem(y + NY - 1, NY)

    def at_z(step):
        return lax.rem(z + step + NZ, NZ)

    def at_ctx(x_step, core_step):
        return lax.rem(x + x_step, NX) * 2 + lax.rem(core + core_step, 2)

    barrier = pltpu.get_barrier_semaphore()
    line = [(at_z(step) * NY + y, ctx) for step in (1, -1, 2, -2, 4)]
    near = [(dp, at_ctx(x_step, core_step)) for x_step in range(NX) for core_step in range(2)
            if x_step or core_step]
    for dev in line + near + [(left, ctx), (right, ctx)]:
        pl.semaphore_signal(barrier, inc=1, device_id=dev, device_id_type=MESH)

    places = [rank(lax.rem(y0 - y + NY, NY)) for y0 in range(NY)]

    def order_rows(home, carry):
        for head in range(KV_HEADS):
            for which, source in enumerate((queries, grads)):
                block = source[pl.ds(pl.multiple_of(home * 16, 16), 16),
                               head * GROUP * HEAD_DIM:(head + 1) * GROUP * HEAD_DIM]
                block = block.reshape(16, GROUP, HEAD_DIM)
                for y0 in range(NY):
                    rows[head * NZ + home, places[y0], which] = block[2 * y0:2 * y0 + 2]
        return carry

    pos = positions[...]
    spot = lax.broadcasted_iota(jnp.int32, (8, HALF), 0)
    first_rows = []
    for s in range(SUBS):
        line_pos = pos[s:s + 1, :]
        first = jnp.zeros_like(line_pos)
        end = jnp.int32(0)
        for doc in range(8):
            end = end + lengths[s, doc]
            first = jnp.where(line_pos >= end, end, first)
        first_rows.append(first)
    table = jnp.zeros((8, HALF), jnp.int32)
    for s in range(SUBS):
        for part, line_value in enumerate((pos[s:s + 1, :], first_rows[s])):
            high = lax.shift_right_logical(line_value, 4)
            table = jnp.where(spot == s * 4 + part * 2, high, table)
            table = jnp.where(spot == s * 4 + part * 2 + 1, line_value - high * 16, table)
    table = table.astype(jnp.float32).astype(jnp.bfloat16)
    lane8 = lax.broadcasted_iota(jnp.int32, (8, 128), 1)
    row8 = lax.broadcasted_iota(jnp.int32, (8, 128), 0)
    lane64 = lax.broadcasted_iota(jnp.int32, (HALF, 128), 1)
    row64 = lax.broadcasted_iota(jnp.int32, (HALF, 128), 0)
    wanted = lax.rem(lax.div(lane8, 32), 2) * 4 + lax.rem(lane8, 4)

    for copy in range(2):
        marks = []
        for e_hi in range(2):
            low, high = [at_z(4 * copy + z_step(2 * e_hi + e_lo, core)) for e_lo in range(2)]
            source = jnp.where(lane64 < 64, low, high) * NY + lax.rem(lax.div(lane64, 4), NY)
            pick_rows = (row64 == source).astype(jnp.float32).astype(jnp.bfloat16)
            found = jnp.dot(table, pick_rows, preferred_element_type=jnp.float32)
            found = jnp.sum(jnp.where(row8 == wanted, found, 0.0), axis=0, keepdims=True)
            marks.append(jnp.broadcast_to(found, (GROUP, 128)))
        marks = jnp.concatenate(marks, axis=0).astype(jnp.bfloat16)
        for head in range(KV_HEADS):
            cols = slice(head * HEAD_DIM, (head + 1) * HEAD_DIM)
            kv_out[copy, head, 0:128] = keys[:, cols]
            kv_out[copy, head, 128:256] = values[:, cols]
            kv_out[copy, head, 256:272] = marks

    lax.fori_loop(0, NZ, order_rows, 0)

    pl.semaphore_wait(barrier, len(line) + len(near) + 2)
    for dev in line:
        pl.semaphore_signal(second, inc=1, device_id=dev, device_id_type=MESH)
    pl.semaphore_wait(second, len(line))

    def remote(src, dst, send, recv, dev):
        return pltpu.make_async_remote_copy(src_ref=src, dst_ref=dst, send_sem=send, recv_sem=recv,
                                            device_id=dev, device_id_type=MESH)

    def wait_bytes(ref, sem):
        pltpu.make_async_copy(ref, ref, sem).wait()

    here = kv.at[y, ctx]
    for x_step in (1, 3, 2):
        head = lax.rem(x + x_step, NX)
        remote(kv_out.at[0, head], here, kva_send, kv_recv, (dp, head * 2)).start()

    @pl.when(core == 0)
    def _():
        pltpu.make_async_copy(kv_out.at[0, x], here, kv_recv).start()

    @pl.when(core != 0)
    def _():
        remote(kv_out.at[0, x], here, kva_send, kv_recv, (dp, x * 2)).start()

    far = at_z(4) * NY + y
    for x_step in (1, 3, 2, 0):
        head = lax.rem(x + x_step, NX)
        remote(kv_out.at[1, head], here, kvb_send, kv_recv, (far, head * 2 + 1)).start()

    def send_rows(part):
        ranks = pl.ds(0, EARLY) if part == 0 else pl.ds(EARLY, PLACES - EARLY)
        for e in (0, 2, 3, 1):
            server_z = at_z(-z_step(e, core))
            for other in range(2):
                copy = lax.rem(core + other, 2)
                home = lax.rem(server_z + 4 * copy, NZ)
                for x_step in (1, 3, 2, 0):
                    head = lax.rem(x + x_step, NX)
                    src = rows.at[head * NZ + home, ranks]
                    dst = got.at[(e % 2) * 16 + ctx * 2 + e // 2, ranks]
                    if e == 1 and other == 0 and x_step == 0:
                        pltpu.make_async_copy(src, dst, row_recv.at[part]).start()
                    else:
                        remote(src, dst, row_send.at[part], row_recv.at[part],
                               (server_z * NY + y, head * 2 + copy)).start()

    def ring(step):
        from_left = kv.at[lax.rem(y - step + NY, NY)]
        from_right = kv.at[lax.rem(y + step, NY)]
        if step == 3:
            from_left = from_left.at[pl.ds(0, 4)]
            from_right = from_right.at[pl.ds(4, 4)]
        return (remote(from_left, from_left, ring_send.at[0, step], ring_recv.at[0, step], (right, ctx)),
                remote(from_right, from_right, ring_send.at[1, step], ring_recv.at[1, step], (left, ctx)))

    def ring_start(step):
        for copy in ring(step):
            copy.start()

    def ring_arrived(step):
        from_left = kv.at[lax.rem(y - step - 1 + NY, NY)]
        from_right = kv.at[lax.rem(y + step + 1, NY)]
        if step == 3:
            from_left = from_left.at[pl.ds(0, 4)]
            from_right = from_right.at[pl.ds(4, 4)]
        wait_bytes(from_left, ring_recv.at[0, step])
        wait_bytes(from_right, ring_recv.at[1, step])

    send_rows(0)

    @pl.when(core == 0)
    def _():
        wait_bytes(kv.at[y], kv_recv)
        ring_start(0)

    send_rows(1)

    @pl.when(core != 0)
    def _():
        wait_bytes(kv.at[y], kv_recv)
        ring_start(0)

    scale = 1.0 / math.sqrt(HEAD_DIM)
    to_log2 = scale * math.log2(math.e)
    lane = lax.broadcasted_iota(jnp.int32, (128, 128), 0)
    key_pos = lax.broadcasted_iota(jnp.int32, (256, SEQ), 1).astype(jnp.float32)
    lse_lane = lax.broadcasted_iota(jnp.int32, (256, 128), 1)
    server_home = at_z(4 * core)

    def pick(base):
        return jnp.where(lane == base, 16.0, jnp.where(lane == base + 1, 1.0, 0.0)).astype(jnp.bfloat16)

    def dot(a, b, dims):
        return lax.dot_general(a, b, (dims, ((), ())), preferred_element_type=jnp.float32)

    def one_sequence(n, y0, s):
        q = got[:, n, 0, s].reshape(256, HEAD_DIM)
        g = got[:, n, 1, s].reshape(256, HEAD_DIM)
        k = kv[y0, :, pl.ds(pl.multiple_of(s * HALF, HALF), HALF), :].reshape(SEQ, HEAD_DIM)
        v = kv[y0, :, pl.ds(pl.multiple_of(128 + s * HALF, HALF), HALF), :].reshape(SEQ, HEAD_DIM)
        marks = kv[y0, :, pl.ds(256, 16), :].reshape(128, 128)
        bounds = []
        for which in range(2):
            halves = [dot(marks, pick(e_lo * 64 + s * 32 + y * 4 + which * 2), ((1,), (0,)))
                      for e_lo in range(2)]
            whole = jnp.concatenate(halves, axis=0)
            bounds.append(jnp.concatenate([whole] * 4, axis=1))
        visible = jnp.logical_and(key_pos <= bounds[0], key_pos >= bounds[1])
        scores = jnp.where(visible, dot(q, k, ((1,), (1,))) * to_log2, NEG_FILL)
        top = jnp.max(scores, axis=1, keepdims=True)
        p = jnp.exp2(scores - top)
        total = jnp.sum(p, axis=1, keepdims=True)
        inverse = 1.0 / total
        att = (dot(p.astype(jnp.bfloat16), v, ((1,), (0,))) * inverse).astype(jnp.bfloat16)
        delta = jnp.sum(g.astype(jnp.float32) * att.astype(jnp.float32), axis=1, keepdims=True)
        grad = dot(g, v, ((1,), (1,)))
        ds = (p * (grad - delta)).astype(jnp.bfloat16)
        dq = (dot(ds, k, ((1,), (0,))) * (inverse * scale)).astype(jnp.bfloat16)
        res[:, n * 4 + s] = att.reshape(SLOTS, GROUP, HEAD_DIM)
        res[:, n * 4 + 2 + s] = dq.reshape(SLOTS, GROUP, HEAD_DIM)
        left_over = (top + jnp.log2(total)) * math.log(2.0)
        kept = lse[...]
        for part in range(3):
            term = left_over.astype(jnp.bfloat16).astype(jnp.float32)
            left_over = left_over - term
            kept = jnp.where(lse_lane == part * 16 + y0 * SUBS + s, term, kept)
        lse[...] = kept

    def serve(n, carry):
        y0 = lax.rem(y + lax.div(n + 1, 2) * (2 * lax.rem(n, 2) - 1) + NY, NY)

        def sub(s, inner):
            one_sequence(n, y0, s)
            return inner

        return lax.fori_loop(0, SUBS, sub, carry)

    def give(lower, upper):
        tiles = pl.ds(lower * 4, (upper - lower) * 4 + (1 if upper == PLACES else 0))
        dst = out.at[x, server_home, tiles]
        for e in (0, 2, 3, 1):
            for other in range(2):
                home_core = lax.rem(core + other, 2)
                home_z = at_z(z_step(e, home_core))
                for x_step in (1, 3, 2, 0):
                    home_ctx = lax.rem(x + x_step, NX) * 2 + home_core
                    src = res.at[(e % 2) * 16 + home_ctx * 2 + e // 2, tiles]
                    if e == 1 and other == 0 and x_step == 0:
                        pltpu.make_async_copy(src, dst, res_recv).start()
                    else:
                        remote(src, dst, res_send, res_recv, (home_z * NY + y, home_ctx)).start()

    lse[...] = jnp.zeros_like(lse)
    ring_arrived(0)
    ring_start(1)
    wait_bytes(got.at[:, pl.ds(0, EARLY)], row_recv.at[0])
    lax.fori_loop(0, 3, serve, 0)
    give(0, 3)
    ring_arrived(1)
    ring_start(2)
    wait_bytes(got.at[:, pl.ds(EARLY, PLACES - EARLY)], row_recv.at[1])
    lax.fori_loop(3, 5, serve, 0)
    give(3, 5)
    ring_arrived(2)
    ring_start(3)
    lax.fori_loop(5, 7, serve, 0)
    give(5, 7)
    ring_arrived(3)
    lax.fori_loop(7, 8, serve, 0)
    res[:, 4 * PLACES] = lse[...].astype(jnp.bfloat16).reshape(SLOTS, GROUP, 128)
    give(7, 8)

    sent = pl.ds(0, SLOTS - 1)
    wait_bytes(rows.at[sent, pl.ds(0, EARLY)], row_send.at[0])
    wait_bytes(rows.at[sent, pl.ds(EARLY, PLACES - EARLY)], row_send.at[1])
    wait_bytes(kv.at[0, pl.ds(0, 4)], kvb_send)

    @pl.when(core == 0)
    def _():
        wait_bytes(kv.at[0, pl.ds(0, 3)], kva_send)

    @pl.when(core != 0)
    def _():
        wait_bytes(kv.at[0, pl.ds(0, 4)], kva_send)

    for step in range(4):
        for copy in ring(step):
            copy.wait_send()
    wait_bytes(res.at[sent], res_send)
    wait_bytes(out, res_recv)


def order_results(got, attended, lse, grad):
    home = pl.program_id(0)
    y = lax.rem(lax.axis_index("dp"), NY)
    for head in range(KV_HEADS):
        cols = slice(head * GROUP * HEAD_DIM, (head + 1) * GROUP * HEAD_DIM)
        for which, result in enumerate((attended, grad)):
            pairs = [got[head, 0, pl.ds(4 * rank(lax.rem(y0 - y + NY, NY)) + 2 * which, 2)]
                     for y0 in range(NY)]
            result[:, cols] = jnp.concatenate(pairs, axis=0).reshape(16, GROUP * HEAD_DIM)
    terms = got[:, 0, 4 * PLACES].reshape(HEADS, 128).astype(jnp.float32)
    total = terms + pltpu.roll(terms, 112, 1) + pltpu.roll(terms, 96, 1)
    lane = lax.broadcasted_iota(jnp.int32, (HEADS, 128), 1)
    total = pltpu.roll(jnp.where(lane < 16, total, 0.0), home * 16, 1)

    @pl.when(home == 0)
    def _():
        lse[...] = total

    @pl.when(home != 0)
    def _():
        lse[...] = lse[...] + total


def local(queries, key_rows, value_rows, out_grad, doc_lengths, served_positions):
    bf16 = jnp.bfloat16
    dma = pltpu.SemaphoreType.DMA
    vmem = pl.BlockSpec(memory_space=pltpu.VMEM)
    result = pl.pallas_call(
        kernel,
        out_shape=jax.ShapeDtypeStruct((KV_HEADS, NZ, TILES, GROUP, HEAD_DIM), bf16),
        in_specs=[vmem, vmem, vmem, vmem, pl.BlockSpec(memory_space=pltpu.SMEM), vmem],
        out_specs=pl.BlockSpec(memory_space=pl.ANY),
        scratch_shapes=[
            pltpu.VMEM((SLOTS, PLACES, 2, SUBS, GROUP, HEAD_DIM), bf16),
            pltpu.VMEM((2, KV_HEADS, KV_ROWS, HEAD_DIM), bf16),
            pltpu.VMEM((NY, NCTX, KV_ROWS, HEAD_DIM), bf16),
            pltpu.VMEM((SLOTS, PLACES, 2, SUBS, GROUP, HEAD_DIM), bf16),
            pltpu.VMEM((SLOTS, TILES, GROUP, HEAD_DIM), bf16),
            pltpu.VMEM((SLOTS * GROUP, 128), jnp.float32),
            pltpu.SemaphoreType.REGULAR,
            dma((2,)), dma((2,)), dma, dma, dma, dma((2, 4)), dma((2, 4)), dma, dma,
        ],
        compiler_params=pltpu.CompilerParams(
            collective_id=0, has_side_effects=True, vmem_limit_bytes=48 * 1024 * 1024
        ),
        cost_estimate=pl.CostEstimate(flops=4 * 10**9, bytes_accessed=8 * 2**20,
                                      transcendentals=2 * 2**20),
    )(queries, out_grad, key_rows, value_rows, doc_lengths,
      served_positions.reshape(NZ * NY, SUBS).T)

    wide = HEADS * HEAD_DIM
    attended, lse, grad = pl.pallas_call(
        order_results,
        grid=(NZ,),
        out_shape=(
            jax.ShapeDtypeStruct((NZ * 16, wide), bf16),
            jax.ShapeDtypeStruct((HEADS, 128), jnp.float32),
            jax.ShapeDtypeStruct((NZ * 16, wide), bf16),
        ),
        in_specs=[pl.BlockSpec((KV_HEADS, 1, TILES, GROUP, HEAD_DIM), lambda i: (0, i, 0, 0, 0))],
        out_specs=(
            pl.BlockSpec((16, wide), lambda i: (i, 0)),
            pl.BlockSpec((HEADS, 128), lambda i: (0, 0)),
            pl.BlockSpec((16, wide), lambda i: (i, 0)),
        ),
        cost_estimate=pl.CostEstimate(flops=0, bytes_accessed=4 * 2**20, transcendentals=0),
    )(result)
    return attended, lse.T, grad


def solution(mesh):
    in_specs = (
        P(("dp", "ctx"), None),
        P(("dp", "ctx"), None),
        P(("dp", "ctx"), None),
        P(("dp", "ctx"), None),
        P("dp", None),
        P("dp", "ctx", None, None),
    )
    out_specs = (P(("dp", "ctx"), None), P(("dp", "ctx"), None), P(("dp", "ctx"), None))
    return jax.shard_map(local, mesh=mesh, in_specs=in_specs, out_specs=out_specs, check_vma=False)
```

```python
import functools
import math

import jax
import jax.numpy as jnp
from jax import lax
from jax.experimental import pallas as pl
from jax.experimental.pallas import tpu as pltpu
from jax.sharding import PartitionSpec as P

HEAD_DIM = 128
HEADS = 32
KV_HEADS = 4
GROUP = HEADS // KV_HEADS
SUBS = 2
NZ = 8
NY = 8
NX = 4
NCTX = 8
SLOTS = 32
HALF = 64
SEQ = 512
PLACES = NY
TILES = 4 * PLACES + 1
EARLY = 3
STEPS = (0, 1, 3, 2)
KV_ROWS = 272
NEG_FILL = -1e30
MESH = pl.DeviceIdType.MESH


def y_step(e, core):
    return e - 1 - 4 * core * (e // 3)


def rank(distance):
    return jnp.where(distance <= 4, jnp.maximum(2 * distance - 1, 0), 16 - 2 * distance)


def kernel(queries, grads, keys, values, lengths, positions, out,
           query_in, grad_in, key_in, value_in, lengths_in, positions_in,
           rows, kv_out, kv, got, res, lse, second,
           load, small_load, row_send, row_recv, kva_send, kvb_send, kv_recv, ring_send, ring_recv,
           res_send, res_recv):
    dp = lax.axis_index("dp")
    ctx = lax.axis_index("ctx")
    z, y = lax.div(dp, NY), lax.rem(dp, NY)
    x, core = lax.div(ctx, 2), lax.rem(ctx, 2)
    right = lax.rem(z + 1, NZ) * NY + y
    left = lax.rem(z + NZ - 1, NZ) * NY + y

    def at_y(step):
        return lax.rem(y + step + NY, NY)

    def at_ctx(x_step, core_step):
        return lax.rem(x + x_step, NX) * 2 + lax.rem(core + core_step, 2)

    barrier = pltpu.get_barrier_semaphore()
    line = [(z * NY + at_y(step), ctx) for step in (1, -1, 2, -2, 4)]
    near = [(dp, at_ctx(x_step, core_step)) for x_step in range(NX) for core_step in range(2)
            if x_step or core_step]
    for dev in line + near + [(left, ctx), (right, ctx)]:
        pl.semaphore_signal(barrier, inc=1, device_id=dev, device_id_type=MESH)

    def load_rows(home_z, which):
        block = pl.ds(home_z * 16, 16)
        source, target = ((queries, query_in), (grads, grad_in))[which]
        return pltpu.make_async_copy(source.at[block], target.at[block], load.at[which, home_z])

    small = [pltpu.make_async_copy(source, target, small_load.at[i])
             for i, (source, target) in enumerate(((lengths, lengths_in), (positions, positions_in),
                                                   (keys, key_in), (values, value_in)))]
    for copy in small:
        copy.start()
    for home_z in range(NZ):
        for which in range(2):
            load_rows(home_z, which).start()
    for copy in small:
        copy.wait()

    def order_rows(home_z, carry):
        place = rank(lax.rem(home_z - z + NZ, NZ))
        lines = pl.ds(pl.multiple_of(home_z * 16, 16), 16)
        for which, source in enumerate((query_in, grad_in)):
            load_rows(home_z, which).wait()
            for head in range(KV_HEADS):
                block = source[lines, head * GROUP * HEAD_DIM:(head + 1) * GROUP * HEAD_DIM]
                block = block.reshape(16, GROUP, HEAD_DIM)
                for home_y in range(NY):
                    rows[head * NY + home_y, place, which] = block[2 * home_y:2 * home_y + 2]
        return carry

    pos = positions_in[...]
    spans = lengths_in[...]
    doc_lane = lax.broadcasted_iota(jnp.int32, (SUBS, 8), 1)
    first = jnp.zeros_like(pos)
    for doc in range(8):
        end = jnp.sum(jnp.where(doc_lane <= doc, spans, 0), axis=1, keepdims=True)
        first = jnp.where(pos >= end, end, first)
    spot = lax.broadcasted_iota(jnp.int32, (8, HALF), 0)
    table = jnp.zeros((8, HALF), jnp.int32)
    for s in range(SUBS):
        for part, line_value in enumerate((pos[s:s + 1, :], first[s:s + 1, :])):
            high = lax.shift_right_logical(line_value, 4)
            table = jnp.where(spot == s * 4 + part * 2, high, table)
            table = jnp.where(spot == s * 4 + part * 2 + 1, line_value - high * 16, table)
    table = table.astype(jnp.float32).astype(jnp.bfloat16)
    lane8 = lax.broadcasted_iota(jnp.int32, (8, 128), 1)
    row8 = lax.broadcasted_iota(jnp.int32, (8, 128), 0)
    lane64 = lax.broadcasted_iota(jnp.int32, (HALF, 128), 1)
    row64 = lax.broadcasted_iota(jnp.int32, (HALF, 128), 0)
    wanted = lax.rem(lax.div(lane8, 32), 2) * 4 + lax.rem(lane8, 4)

    for copy in range(2):
        marks = []
        for e_hi in range(2):
            low, high = [at_y(4 * copy + y_step(2 * e_hi + e_lo, core)) for e_lo in range(2)]
            source = jnp.where(lane64 < 64, low, high) + lax.rem(lax.div(lane64, 4), NZ) * NY
            pick_rows = (row64 == source).astype(jnp.float32).astype(jnp.bfloat16)
            found = jnp.dot(table, pick_rows, preferred_element_type=jnp.float32)
            found = jnp.sum(jnp.where(row8 == wanted, found, 0.0), axis=0, keepdims=True)
            marks.append(jnp.broadcast_to(found, (GROUP, 128)))
        marks = jnp.concatenate(marks, axis=0).astype(jnp.bfloat16)
        for head in range(KV_HEADS):
            cols = slice(head * HEAD_DIM, (head + 1) * HEAD_DIM)
            kv_out[copy, head, 0:128] = key_in[:, cols]
            kv_out[copy, head, 128:256] = value_in[:, cols]
            kv_out[copy, head, 256:272] = marks

    lax.fori_loop(0, NZ, order_rows, 0)

    pl.semaphore_wait(barrier, len(line) + len(near) + 2)
    for dev in line:
        pl.semaphore_signal(second, inc=1, device_id=dev, device_id_type=MESH)
    pl.semaphore_wait(second, len(line))

    def remote(src, dst, send, recv, dev):
        return pltpu.make_async_remote_copy(src_ref=src, dst_ref=dst, send_sem=send, recv_sem=recv,
                                            device_id=dev, device_id_type=MESH)

    def wait_bytes(ref, sem):
        pltpu.make_async_copy(ref, ref, sem).wait()

    here = kv.at[z, ctx]
    arrived = kv_recv.at[x]

    @pl.when(core == 0)
    def _():
        pltpu.make_async_copy(kv_out.at[0, x], here, arrived).start()

    @pl.when(core != 0)
    def _():
        remote(kv_out.at[0, x], here, kva_send, arrived, (dp, x * 2)).start()

    far = z * NY + at_y(4)
    remote(kv_out.at[1, x], here, kvb_send, arrived, (far, x * 2 + 1)).start()
    for x_step in STEPS[1:]:
        head = lax.rem(x + x_step, NX)
        remote(kv_out.at[0, head], here, kva_send, arrived, (dp, head * 2)).start()
        remote(kv_out.at[1, head], here, kvb_send, arrived, (far, head * 2 + 1)).start()

    def send_rows(part, which_e):
        ranks = pl.ds(0, EARLY) if part == 0 else pl.ds(EARLY, PLACES - EARLY)
        for e in which_e:
            server_y = at_y(-y_step(e, core))
            for other in range(2):
                copy = lax.rem(core + other, 2)
                home = lax.rem(server_y + 4 * copy, NY)
                for x_step in (1, 3, 2, 0):
                    head = lax.rem(x + x_step, NX)
                    src = rows.at[head * NY + home, ranks]
                    dst = got.at[(e % 2) * 16 + ctx * 2 + e // 2, ranks]
                    if e == 1 and other == 0 and x_step == 0:
                        pltpu.make_async_copy(src, dst, row_recv.at[part]).start()
                    else:
                        remote(src, dst, row_send.at[part], row_recv.at[part],
                               (z * NY + server_y, head * 2 + copy)).start()

    def piece(chunk, i):
        return kv.at[chunk, pl.ds(lax.rem(x + STEPS[i], NX) * 2, 2)]

    def from_left(step):
        return lax.rem(z - step + NZ, NZ)

    def from_right(step):
        return lax.rem(z + step, NZ)

    def pieces(step, way):
        return range(NX) if step < 3 else range(2 * way, 2 * way + 2)

    def forward(step, i):
        if i in pieces(step, 0):
            block = piece(from_left(step), i)
            remote(block, block, ring_send.at[0, step], ring_recv.at[0, step, i], (right, ctx)).start()
        if i in pieces(step, 1):
            block = piece(from_right(step), i)
            remote(block, block, ring_send.at[1, step], ring_recv.at[1, step, i], (left, ctx)).start()

    def begin_ring(i):
        wait_bytes(piece(z, i), kv_recv.at[lax.rem(x + STEPS[i], NX)])
        forward(0, i)

    def pass_on(step):
        for i in range(NX):
            if i in pieces(step, 0):
                wait_bytes(piece(from_left(step + 1), i), ring_recv.at[0, step, i])
            if i in pieces(step, 1):
                wait_bytes(piece(from_right(step + 1), i), ring_recv.at[1, step, i])
            if step < 3:
                forward(step + 1, i)

    send_rows(0, (0, 2, 3, 1))
    begin_ring(0)
    send_rows(1, (0,))
    begin_ring(1)
    send_rows(1, (2,))
    begin_ring(2)
    send_rows(1, (3,))
    begin_ring(3)
    send_rows(1, (1,))

    scale = 1.0 / math.sqrt(HEAD_DIM)
    to_log2 = scale * math.log2(math.e)
    lane = lax.broadcasted_iota(jnp.int32, (128, 128), 0)
    key_pos = lax.broadcasted_iota(jnp.int32, (256, SEQ), 1).astype(jnp.float32)
    lse_lane = lax.broadcasted_iota(jnp.int32, (256, 128), 1)
    server_home = at_y(4 * core)

    def pick(base):
        return jnp.where(lane == base, 16.0, jnp.where(lane == base + 1, 1.0, 0.0)).astype(jnp.bfloat16)

    def dot(a, b, dims):
        return lax.dot_general(a, b, (dims, ((), ())), preferred_element_type=jnp.float32)

    def one_sequence(n, chunk, s):
        q = got[:, n, 0, s].reshape(256, HEAD_DIM)
        g = got[:, n, 1, s].reshape(256, HEAD_DIM)
        k = kv[chunk, :, pl.ds(pl.multiple_of(s * HALF, HALF), HALF), :].reshape(SEQ, HEAD_DIM)
        v = kv[chunk, :, pl.ds(pl.multiple_of(128 + s * HALF, HALF), HALF), :].reshape(SEQ, HEAD_DIM)
        marks = kv[chunk, :, pl.ds(256, 16), :].reshape(128, 128)
        bounds = []
        for which in range(2):
            halves = [dot(marks, pick(e_lo * 64 + s * 32 + z * 4 + which * 2), ((1,), (0,)))
                      for e_lo in range(2)]
            whole = jnp.concatenate(halves, axis=0)
            bounds.append(jnp.concatenate([whole] * 4, axis=1))
        visible = jnp.logical_and(key_pos <= bounds[0], key_pos >= bounds[1])
        scores = jnp.where(visible, dot(q, k, ((1,), (1,))) * to_log2, NEG_FILL)
        top = jnp.max(scores, axis=1, keepdims=True)
        p = jnp.exp2(scores - top)
        total = jnp.sum(p, axis=1, keepdims=True)
        inverse = 1.0 / total
        att = (dot(p.astype(jnp.bfloat16), v, ((1,), (0,))) * inverse).astype(jnp.bfloat16)
        delta = jnp.sum(g.astype(jnp.float32) * att.astype(jnp.float32), axis=1, keepdims=True)
        grad = dot(g, v, ((1,), (1,)))
        ds = (p * (grad - delta)).astype(jnp.bfloat16)
        dq = (dot(ds, k, ((1,), (0,))) * (inverse * scale)).astype(jnp.bfloat16)
        res[:, n * 4 + s] = att.reshape(SLOTS, GROUP, HEAD_DIM)
        res[:, n * 4 + 2 + s] = dq.reshape(SLOTS, GROUP, HEAD_DIM)
        left_over = (top + jnp.log2(total)) * math.log(2.0)
        kept = lse[...]
        for part in range(3):
            term = left_over.astype(jnp.bfloat16).astype(jnp.float32)
            left_over = left_over - term
            kept = jnp.where(lse_lane == part * 16 + chunk * SUBS + s, term, kept)
        lse[...] = kept

    def serve(n, carry):
        chunk = lax.rem(z + lax.div(n + 1, 2) * (2 * lax.rem(n, 2) - 1) + NZ, NZ)

        def sub(s, inner):
            one_sequence(n, chunk, s)
            return inner

        return lax.fori_loop(0, SUBS, sub, carry)

    def give(lower, upper):
        tiles = pl.ds(lower * 4, (upper - lower) * 4 + (1 if upper == PLACES else 0))
        dst = out.at[x, server_home, tiles]
        for e in (0, 2, 3, 1):
            for other in range(2):
                home_core = lax.rem(core + other, 2)
                home_y = at_y(y_step(e, home_core))
                for x_step in (1, 3, 2, 0):
                    home_ctx = lax.rem(x + x_step, NX) * 2 + home_core
                    src = res.at[(e % 2) * 16 + home_ctx * 2 + e // 2, tiles]
                    if e == 1 and other == 0 and x_step == 0:
                        pltpu.make_async_copy(src, dst, res_recv).start()
                    else:
                        remote(src, dst, res_send, res_recv, (z * NY + home_y, home_ctx)).start()

    lse[...] = jnp.zeros_like(lse)
    pass_on(0)
    wait_bytes(got.at[:, pl.ds(0, EARLY)], row_recv.at[0])
    lax.fori_loop(0, 3, serve, 0)
    give(0, 3)
    pass_on(1)
    wait_bytes(got.at[:, pl.ds(EARLY, PLACES - EARLY)], row_recv.at[1])
    lax.fori_loop(3, 5, serve, 0)
    give(3, 5)
    pass_on(2)
    lax.fori_loop(5, 7, serve, 0)
    give(5, 7)
    pass_on(3)
    lax.fori_loop(7, 8, serve, 0)
    res[:, 4 * PLACES] = lse[...].astype(jnp.bfloat16).reshape(SLOTS, GROUP, 128)
    give(7, 8)

    sent = pl.ds(0, SLOTS - 1)
    wait_bytes(rows.at[sent, pl.ds(0, EARLY)], row_send.at[0])
    wait_bytes(rows.at[sent, pl.ds(EARLY, PLACES - EARLY)], row_send.at[1])
    wait_bytes(kv.at[0, pl.ds(0, 4)], kvb_send)

    @pl.when(core == 0)
    def _():
        wait_bytes(kv.at[0, pl.ds(0, 3)], kva_send)

    @pl.when(core != 0)
    def _():
        wait_bytes(kv.at[0, pl.ds(0, 4)], kva_send)

    for step in range(4):
        for way in range(2):
            wait_bytes(kv.at[0] if step < 3 else kv.at[0, pl.ds(0, 4)], ring_send.at[way, step])
    wait_bytes(res.at[sent], res_send)
    wait_bytes(out, res_recv)


def order_results(got, attended, lse, grad, held, attended_rows, lse_rows, grad_rows,
                  load, store, lse_store):
    z = lax.div(lax.axis_index("dp"), NY)

    def load_part(n):
        tiles = pl.ds(4 * n, 4) if n < PLACES else pl.ds(4 * PLACES, 1)
        return pltpu.make_async_copy(got.at[:, :, tiles], held.at[:, :, tiles], load.at[n])

    def store_part(n, which):
        chunk = lax.rem(z + ((n + 1) // 2) * (2 * (n % 2) - 1) + NZ, NZ)
        lines = pl.ds(pl.multiple_of(chunk * 16, 16), 16)
        source, target = ((attended_rows, attended), (grad_rows, grad))[which]
        return lines, source, pltpu.make_async_copy(source.at[lines], target.at[lines], store.at[which, n])

    order = [PLACES] + list(range(PLACES))
    for n in order:
        load_part(n).start()
    load_part(PLACES).wait()
    column = lax.broadcasted_iota(jnp.int32, (128, 128), 1)
    source = lax.broadcasted_iota(jnp.int32, (128, 128), 0)
    target = lax.div(lax.rem(source, 16), 2) * 16 + lax.rem(source, 2)
    target = jnp.where(source < 48, target, -128)
    total = jnp.zeros((HEADS, 128), jnp.float32)
    for home_y in range(NY):
        terms = held[:, home_y, 4 * PLACES].reshape(HEADS, 128)
        place = (column == target + home_y * SUBS).astype(jnp.float32).astype(jnp.bfloat16)
        total = total + jnp.dot(terms, place, preferred_element_type=jnp.float32)
    lse_rows[...] = total
    lse_copy = pltpu.make_async_copy(lse_rows, lse, lse_store)
    lse_copy.start()
    for n in range(PLACES):
        load_part(n).wait()
        for which in range(2):
            lines, result, copy = store_part(n, which)
            for head in range(KV_HEADS):
                cols = slice(head * GROUP * HEAD_DIM, (head + 1) * GROUP * HEAD_DIM)
                block = held[head, :, 4 * n + 2 * which:4 * n + 2 * which + 2]
                result[lines, cols] = block.reshape(16, GROUP * HEAD_DIM)
            copy.start()
    for n in range(PLACES):
        for which in range(2):
            store_part(n, which)[2].wait()
    lse_copy.wait()


def local(queries, key_rows, value_rows, out_grad, doc_lengths, served_positions):
    bf16 = jnp.bfloat16
    dma = pltpu.SemaphoreType.DMA
    hbm = pl.BlockSpec(memory_space=pltpu.HBM)
    wide = HEADS * HEAD_DIM
    thin = KV_HEADS * HEAD_DIM
    result = pl.pallas_call(
        kernel,
        out_shape=jax.ShapeDtypeStruct((KV_HEADS, NY, TILES, GROUP, HEAD_DIM), bf16),
        in_specs=[hbm] * 6,
        out_specs=hbm,
        scratch_shapes=[
            pltpu.VMEM((NZ * 16, wide), bf16),
            pltpu.VMEM((NZ * 16, wide), bf16),
            pltpu.VMEM((128, thin), bf16),
            pltpu.VMEM((128, thin), bf16),
            pltpu.VMEM((SUBS, 8), jnp.int32),
            pltpu.VMEM((SUBS, HALF), jnp.int32),
            pltpu.VMEM((SLOTS, PLACES, 2, SUBS, GROUP, HEAD_DIM), bf16),
            pltpu.VMEM((2, KV_HEADS, KV_ROWS, HEAD_DIM), bf16),
            pltpu.VMEM((NZ, NCTX, KV_ROWS, HEAD_DIM), bf16),
            pltpu.VMEM((SLOTS, PLACES, 2, SUBS, GROUP, HEAD_DIM), bf16),
            pltpu.VMEM((SLOTS, TILES, GROUP, HEAD_DIM), bf16),
            pltpu.VMEM((SLOTS * GROUP, 128), jnp.float32),
            pltpu.SemaphoreType.REGULAR,
            dma((2, NZ)), dma((4,)), dma((2,)), dma((2,)), dma, dma, dma((NX,)),
            dma((2, 4)), dma((2, 4, NX)), dma, dma,
        ],
        compiler_params=pltpu.CompilerParams(
            collective_id=0, has_side_effects=True, vmem_limit_bytes=48 * 1024 * 1024
        ),
        cost_estimate=pl.CostEstimate(flops=4 * 10**9, bytes_accessed=8 * 2**20,
                                      transcendentals=2 * 2**20),
    )(queries, out_grad, key_rows, value_rows, doc_lengths,
      served_positions.reshape(NZ * NY, SUBS).T)

    attended, lse, grad = pl.pallas_call(
        order_results,
        out_shape=(
            jax.ShapeDtypeStruct((NZ * 16, wide), bf16),
            jax.ShapeDtypeStruct((HEADS, 128), jnp.float32),
            jax.ShapeDtypeStruct((NZ * 16, wide), bf16),
        ),
        in_specs=[hbm],
        out_specs=(hbm, hbm, hbm),
        scratch_shapes=[
            pltpu.VMEM((KV_HEADS, NY, TILES, GROUP, HEAD_DIM), bf16),
            pltpu.VMEM((NZ * 16, wide), bf16),
            pltpu.VMEM((HEADS, 128), jnp.float32),
            pltpu.VMEM((NZ * 16, wide), bf16),
            dma((PLACES + 1,)), dma((2, PLACES)), dma,
        ],
        compiler_params=pltpu.CompilerParams(vmem_limit_bytes=32 * 1024 * 1024),
        cost_estimate=pl.CostEstimate(flops=0, bytes_accessed=4 * 2**20, transcendentals=0),
    )(result)
    return attended, lse.T, grad


def solution(mesh):
    in_specs = (
        P(("dp", "ctx"), None),
        P(("dp", "ctx"), None),
        P(("dp", "ctx"), None),
        P(("dp", "ctx"), None),
        P("dp", None),
        P("dp", "ctx", None, None),
    )
    out_specs = (P(("dp", "ctx"), None), P(("dp", "ctx"), None), P(("dp", "ctx"), None))
    return jax.shard_map(local, mesh=mesh, in_specs=in_specs, out_specs=out_specs, check_vma=False)
```

```python
import functools
import math

import jax
import jax.numpy as jnp
from jax import lax
from jax.experimental import pallas as pl
from jax.experimental.pallas import tpu as pltpu
from jax.sharding import PartitionSpec as P

HEAD_DIM = 128
HEADS = 32
KV_HEADS = 4
GROUP = HEADS // KV_HEADS
SUBS = 2
NZ = 8
NY = 8
NX = 4
NCTX = 8
SLOTS = 32
HALF = 64
SEQ = 512
PLACES = NY
TILES = 4 * PLACES + 1
EARLY = 3
STEPS = (0, 1, 3, 2)
KV_ROWS = 256
NEG_FILL = -1e30
VMEM_BYTES = 63 * 1024 * 1024
MESH = pl.DeviceIdType.MESH


def y_step(e, core):
    return e - 1 - 4 * core * (e // 3)


def rank(distance):
    return jnp.where(distance <= 4, jnp.maximum(2 * distance - 1, 0), 16 - 2 * distance)


def kernel(queries, grads, keys, values, lengths, positions, out,
           query_in, grad_in, key_in, value_in, lengths_in, positions_in,
           rows, kv_out, marks_out, marks_in, marks, bounds, kv, got, res, lse, second,
           load, small_load, row_send, row_recv, kva_send, kvb_send, kv_recv, ring_send, ring_recv,
           marka_send, markb_send, mark_recv, marks_send, marks_recv, res_send, res_recv):
    dp = lax.axis_index("dp")
    ctx = lax.axis_index("ctx")
    z, y = lax.div(dp, NY), lax.rem(dp, NY)
    x, core = lax.div(ctx, 2), lax.rem(ctx, 2)
    right = lax.rem(z + 1, NZ) * NY + y
    left = lax.rem(z + NZ - 1, NZ) * NY + y

    def at_y(step):
        return lax.rem(y + step + NY, NY)

    def at_ctx(x_step, core_step):
        return lax.rem(x + x_step, NX) * 2 + lax.rem(core + core_step, 2)

    def load_small(i):
        source, target = ((keys, key_in), (values, value_in), (lengths, lengths_in),
                          (positions, positions_in))[i]
        return pltpu.make_async_copy(source, target, small_load.at[i])

    for i in range(4):
        load_small(i).start()

    barrier = pltpu.get_barrier_semaphore()
    line = [(z * NY + at_y(step), ctx) for step in (1, -1, 2, -2)]
    near = [(dp, at_ctx(x_step, core_step)) for x_step in range(NX) for core_step in range(2)
            if x_step or core_step]
    far = z * NY + at_y(4)
    opposite = [(far, at_ctx(x_step, core_step)) for x_step in range(NX) for core_step in range(2)]
    ring_line = [(lax.rem(z + step, NZ) * NY + y, ctx) for step in range(1, NZ)]
    first_round = near + opposite + line + ring_line
    for dev in first_round:
        pl.semaphore_signal(barrier, inc=1, device_id=dev, device_id_type=MESH)

    def load_rows(home_z, which):
        block = pl.ds(home_z * 16, 16)
        source, target = ((queries, query_in), (grads, grad_in))[which]
        return pltpu.make_async_copy(source.at[block], target.at[block], load.at[which, home_z])

    for home_z in range(NZ):
        for which in range(2):
            load_rows(home_z, which).start()

    def order_rows(home_z, carry):
        place = rank(lax.rem(home_z - z + NZ, NZ))
        lines = pl.ds(pl.multiple_of(home_z * 16, 16), 16)
        for which, source in enumerate((query_in, grad_in)):
            load_rows(home_z, which).wait()
            for head in range(KV_HEADS):
                block = source[lines, head * GROUP * HEAD_DIM:(head + 1) * GROUP * HEAD_DIM]
                block = block.reshape(16, GROUP, HEAD_DIM)
                for home_y in range(NY):
                    rows[head * NY + home_y, place, which] = block[2 * home_y:2 * home_y + 2]
        return carry

    def remote(src, dst, send, recv, dev):
        return pltpu.make_async_remote_copy(src_ref=src, dst_ref=dst, send_sem=send, recv_sem=recv,
                                            device_id=dev, device_id_type=MESH)

    def wait_bytes(ref, sem):
        pltpu.make_async_copy(ref, ref, sem).wait()

    load_small(0).wait()
    load_small(1).wait()
    for head in range(KV_HEADS):
        cols = slice(head * HEAD_DIM, (head + 1) * HEAD_DIM)
        kv_out[head, 0:128] = key_in[:, cols]
        kv_out[head, 128:256] = value_in[:, cols]

    pl.semaphore_wait(barrier, len(first_round))
    for dev in line:
        pl.semaphore_signal(second, inc=1, device_id=dev, device_id_type=MESH)

    here = kv.at[z, ctx]
    arrived = kv_recv.at[x]

    @pl.when(core == 0)
    def _():
        pltpu.make_async_copy(kv_out.at[x], here, arrived).start()

    @pl.when(core != 0)
    def _():
        remote(kv_out.at[x], here, kva_send, arrived, (dp, x * 2)).start()

    remote(kv_out.at[x], here, kvb_send, arrived, (far, x * 2 + 1)).start()
    for x_step in STEPS[1:]:
        head = lax.rem(x + x_step, NX)
        remote(kv_out.at[head], here, kva_send, arrived, (dp, head * 2)).start()
        remote(kv_out.at[head], here, kvb_send, arrived, (far, head * 2 + 1)).start()

    load_small(2).wait()
    load_small(3).wait()
    pos = positions_in[...]
    spans = lengths_in[...]
    doc_lane = lax.broadcasted_iota(jnp.int32, (SUBS, 8), 1)
    first = jnp.zeros_like(pos)
    for doc in range(8):
        end = jnp.sum(jnp.where(doc_lane <= doc, spans, 0), axis=1, keepdims=True)
        first = jnp.where(pos >= end, end, first)
    spot = lax.broadcasted_iota(jnp.int32, (8, HALF), 0)
    table = jnp.zeros((8, HALF), jnp.int32)
    for s in range(SUBS):
        for part, line_value in enumerate((pos[s:s + 1, :], first[s:s + 1, :])):
            high = lax.shift_right_logical(line_value, 4)
            table = jnp.where(spot == s * 4 + part * 2, high, table)
            table = jnp.where(spot == s * 4 + part * 2 + 1, line_value - high * 16, table)
    table = table.astype(jnp.float32).astype(jnp.bfloat16)
    lane8 = lax.broadcasted_iota(jnp.int32, (8, 128), 1)
    row8 = lax.broadcasted_iota(jnp.int32, (8, 128), 0)
    lane64 = lax.broadcasted_iota(jnp.int32, (HALF, 128), 1)
    row64 = lax.broadcasted_iota(jnp.int32, (HALF, 128), 0)
    wanted = lax.rem(lax.div(lane8, 32), 2) * 4 + lax.rem(lane8, 4)

    for copy in range(2):
        made = []
        for e_hi in range(2):
            low, high = [at_y(4 * copy + y_step(2 * e_hi + e_lo, core)) for e_lo in range(2)]
            source = jnp.where(lane64 < 64, low, high) + lax.rem(lax.div(lane64, 4), NZ) * NY
            pick_rows = (row64 == source).astype(jnp.float32).astype(jnp.bfloat16)
            found = jnp.dot(table, pick_rows, preferred_element_type=jnp.float32)
            found = jnp.sum(jnp.where(row8 == wanted, found, 0.0), axis=0, keepdims=True)
            made.append(jnp.broadcast_to(found, (GROUP, 128)))
        made = jnp.concatenate(made, axis=0).astype(jnp.bfloat16)
        marks_out[copy] = made
    marks_here = marks_in.at[ctx]

    @pl.when(core == 0)
    def _():
        pltpu.make_async_copy(marks_out.at[0], marks_here, mark_recv).start()

    @pl.when(core != 0)
    def _():
        remote(marks_out.at[0], marks_here, marka_send, mark_recv, (dp, x * 2)).start()

    remote(marks_out.at[1], marks_here, markb_send, mark_recv, (far, x * 2 + 1)).start()
    for x_step in STEPS[1:]:
        head = lax.rem(x + x_step, NX)
        remote(marks_out.at[0], marks_here, marka_send, mark_recv, (dp, head * 2)).start()
        remote(marks_out.at[1], marks_here, markb_send, mark_recv, (far, head * 2 + 1)).start()

    def send_rows(part, which_e):
        ranks = pl.ds(0, EARLY) if part == 0 else pl.ds(EARLY, PLACES - EARLY)
        for e in which_e:
            server_y = at_y(-y_step(e, core))
            for other in range(2):
                copy = lax.rem(core + other, 2)
                home = lax.rem(server_y + 4 * copy, NY)
                for x_step in (1, 3, 2, 0):
                    head = lax.rem(x + x_step, NX)
                    src = rows.at[head * NY + home, ranks]
                    dst = got.at[(e % 2) * 16 + ctx * 2 + e // 2, ranks]
                    if e == 1 and other == 0 and x_step == 0:
                        pltpu.make_async_copy(src, dst, row_recv.at[part]).start()
                    else:
                        remote(src, dst, row_send.at[part], row_recv.at[part],
                               (z * NY + server_y, head * 2 + copy)).start()

    def piece(chunk, i):
        return kv.at[chunk, pl.ds(lax.rem(x + STEPS[i], NX) * 2, 2)]

    def from_left(step):
        return lax.rem(z - step + NZ, NZ)

    def from_right(step):
        return lax.rem(z + step, NZ)

    def pieces(step, way):
        return range(NX) if step < 3 else range(2 * way, 2 * way + 2)

    def forward(step, i):
        if i in pieces(step, 0):
            block = piece(from_left(step), i)
            remote(block, block, ring_send.at[0, step], ring_recv.at[0, step, i], (right, ctx)).start()
        if i in pieces(step, 1):
            block = piece(from_right(step), i)
            remote(block, block, ring_send.at[1, step], ring_recv.at[1, step, i], (left, ctx)).start()

    def begin_ring(i):
        wait_bytes(piece(z, i), kv_recv.at[lax.rem(x + STEPS[i], NX)])
        forward(0, i)

    def pass_on(step):
        for i in range(NX):
            if i in pieces(step, 0):
                wait_bytes(piece(from_left(step + 1), i), ring_recv.at[0, step, i])
            if i in pieces(step, 1):
                wait_bytes(piece(from_right(step + 1), i), ring_recv.at[1, step, i])
            if step < 3:
                forward(step + 1, i)

    begin_ring(0)
    lax.fori_loop(0, NZ, order_rows, 0)
    pl.semaphore_wait(second, len(line))
    begin_ring(1)
    send_rows(0, (0, 2))
    begin_ring(2)
    send_rows(0, (3, 1))
    begin_ring(3)
    send_rows(1, (0, 2, 3, 1))

    row16 = lax.broadcasted_iota(jnp.int32, (16, 128), 0)
    col16 = lax.broadcasted_iota(jnp.int32, (16, 128), 1)
    wait_bytes(marks_in, mark_recv)
    thin = (col16 == row16 * GROUP).astype(jnp.float32).astype(jnp.bfloat16)
    marks[z] = jnp.dot(thin, marks_in[...].reshape(128, 128),
                       preferred_element_type=jnp.float32).astype(jnp.bfloat16)
    for dev in ring_line:
        remote(marks.at[z], marks.at[z], marks_send, marks_recv, dev).start()

    scale = 1.0 / math.sqrt(HEAD_DIM)
    to_log2 = scale * math.log2(math.e)
    lane = lax.broadcasted_iota(jnp.int32, (128, 128), 0)
    key_pos = lax.broadcasted_iota(jnp.int32, (256, SEQ), 1).astype(jnp.float32)
    lse_lane = lax.broadcasted_iota(jnp.int32, (256, 128), 1)
    server_home = at_y(4 * core)

    def pick(base):
        return jnp.where(lane == base, 16.0, jnp.where(lane == base + 1, 1.0, 0.0)).astype(jnp.bfloat16)

    def dot(a, b, dims):
        return lax.dot_general(a, b, (dims, ((), ())), preferred_element_type=jnp.float32)

    row128 = lax.broadcasted_iota(jnp.int32, (128, 16), 0)
    col128 = lax.broadcasted_iota(jnp.int32, (128, 16), 1)
    widen = (lax.div(row128, GROUP) == col128).astype(jnp.float32).astype(jnp.bfloat16)

    def make_bounds(chunk, carry):
        wide = jnp.dot(widen, marks[chunk], preferred_element_type=jnp.float32).astype(jnp.bfloat16)
        for s in range(SUBS):
            for which in range(2):
                for e_lo in range(2):
                    base = e_lo * 64 + s * 32 + z * 4 + which * 2
                    bounds[chunk * SUBS + s, which, e_lo * 128:(e_lo + 1) * 128] = dot(
                        wide, pick(base), ((1,), (0,)))
        return carry

    def one_sequence(n, chunk, s):
        q = got[:, n, 0, s].reshape(256, HEAD_DIM)
        g = got[:, n, 1, s].reshape(256, HEAD_DIM)
        k = kv[chunk, :, pl.ds(pl.multiple_of(s * HALF, HALF), HALF), :].reshape(SEQ, HEAD_DIM)
        v = kv[chunk, :, pl.ds(pl.multiple_of(128 + s * HALF, HALF), HALF), :].reshape(SEQ, HEAD_DIM)
        last, first = [jnp.concatenate([bounds[chunk * SUBS + s, which]] * 4, axis=1)
                       for which in range(2)]
        visible = jnp.logical_and(key_pos <= last, key_pos >= first)
        scores = jnp.where(visible, dot(q, k, ((1,), (1,))) * to_log2, NEG_FILL)
        top = jnp.max(scores, axis=1, keepdims=True)
        p = jnp.exp2(scores - top)
        total = jnp.sum(p, axis=1, keepdims=True)
        inverse = 1.0 / total
        att = (dot(p.astype(jnp.bfloat16), v, ((1,), (0,))) * inverse).astype(jnp.bfloat16)
        delta = jnp.sum(g.astype(jnp.float32) * att.astype(jnp.float32), axis=1, keepdims=True)
        grad = dot(g, v, ((1,), (1,)))
        ds = (p * (grad - delta)).astype(jnp.bfloat16)
        dq = (dot(ds, k, ((1,), (0,))) * (inverse * scale)).astype(jnp.bfloat16)
        res[:, n * 4 + s] = att.reshape(SLOTS, GROUP, HEAD_DIM)
        res[:, n * 4 + 2 + s] = dq.reshape(SLOTS, GROUP, HEAD_DIM)
        left_over = (top + jnp.log2(total)) * math.log(2.0)
        kept = lse[...]
        for part in range(3):
            term = left_over.astype(jnp.bfloat16).astype(jnp.float32)
            left_over = left_over - term
            kept = jnp.where(lse_lane == part * 16 + chunk * SUBS + s, term, kept)
        lse[...] = kept

    def serve(n, carry):
        chunk = lax.rem(z + lax.div(n + 1, 2) * (2 * lax.rem(n, 2) - 1) + NZ, NZ)

        def sub(s, inner):
            one_sequence(n, chunk, s)
            return inner

        lax.fori_loop(0, SUBS, sub, 0)
        give(pl.ds(n * 4, 4))
        return carry

    def give(tiles):
        dst = out.at[x, server_home, tiles]
        for e in (0, 2, 3, 1):
            for other in range(2):
                home_core = lax.rem(core + other, 2)
                home_y = at_y(y_step(e, home_core))
                for x_step in (1, 3, 2, 0):
                    home_ctx = lax.rem(x + x_step, NX) * 2 + home_core
                    src = res.at[(e % 2) * 16 + home_ctx * 2 + e // 2, tiles]
                    if e == 1 and other == 0 and x_step == 0:
                        pltpu.make_async_copy(src, dst, res_recv).start()
                    else:
                        remote(src, dst, res_send, res_recv, (z * NY + home_y, home_ctx)).start()

    lse[...] = jnp.zeros_like(lse)
    wait_bytes(marks.at[pl.ds(0, NZ - 1)], marks_recv)
    lax.fori_loop(0, NZ, make_bounds, 0)
    pass_on(0)
    wait_bytes(got.at[:, pl.ds(0, EARLY)], row_recv.at[0])
    lax.fori_loop(0, 3, serve, 0)
    pass_on(1)
    wait_bytes(got.at[:, pl.ds(EARLY, PLACES - EARLY)], row_recv.at[1])
    lax.fori_loop(3, 5, serve, 0)
    pass_on(2)
    lax.fori_loop(5, 7, serve, 0)
    pass_on(3)
    lax.fori_loop(7, 8, serve, 0)
    res[:, 4 * PLACES] = lse[...].astype(jnp.bfloat16).reshape(SLOTS, GROUP, 128)
    give(pl.ds(4 * PLACES, 1))

    sent = pl.ds(0, SLOTS - 1)
    wait_bytes(rows.at[sent, pl.ds(0, EARLY)], row_send.at[0])
    wait_bytes(rows.at[sent, pl.ds(EARLY, PLACES - EARLY)], row_send.at[1])
    wait_bytes(kv.at[0, pl.ds(0, 4)], kvb_send)
    wait_bytes(marks_in.at[pl.ds(0, 4)], markb_send)
    wait_bytes(marks.at[pl.ds(0, NZ - 1)], marks_send)

    @pl.when(core == 0)
    def _():
        wait_bytes(kv.at[0, pl.ds(0, 3)], kva_send)
        wait_bytes(marks_in.at[pl.ds(0, 3)], marka_send)

    @pl.when(core != 0)
    def _():
        wait_bytes(kv.at[0, pl.ds(0, 4)], kva_send)
        wait_bytes(marks_in.at[pl.ds(0, 4)], marka_send)

    for step in range(4):
        for way in range(2):
            wait_bytes(kv.at[0] if step < 3 else kv.at[0, pl.ds(0, 4)], ring_send.at[way, step])
    wait_bytes(res.at[sent], res_send)
    wait_bytes(out, res_recv)


def order_results(got, attended, lse, grad, held, attended_rows, lse_rows, grad_rows,
                  load, store, lse_store):
    z = lax.div(lax.axis_index("dp"), NY)

    def load_part(n):
        tiles = pl.ds(4 * n, 4) if n < PLACES else pl.ds(4 * PLACES, 1)
        return pltpu.make_async_copy(got.at[:, :, tiles], held.at[:, :, tiles], load.at[n])

    def store_part(n, which):
        chunk = lax.rem(z + ((n + 1) // 2) * (2 * (n % 2) - 1) + NZ, NZ)
        lines = pl.ds(pl.multiple_of(chunk * 16, 16), 16)
        source, target = ((attended_rows, attended), (grad_rows, grad))[which]
        return lines, source, pltpu.make_async_copy(source.at[lines], target.at[lines], store.at[which, n])

    order = [PLACES] + list(range(PLACES))
    for n in order:
        load_part(n).start()
    load_part(PLACES).wait()
    column = lax.broadcasted_iota(jnp.int32, (128, 128), 1)
    source = lax.broadcasted_iota(jnp.int32, (128, 128), 0)
    target = lax.div(lax.rem(source, 16), 2) * 16 + lax.rem(source, 2)
    target = jnp.where(source < 48, target, -128)
    total = jnp.zeros((HEADS, 128), jnp.float32)
    for home_y in range(NY):
        terms = held[:, home_y, 4 * PLACES].reshape(HEADS, 128)
        place = (column == target + home_y * SUBS).astype(jnp.float32).astype(jnp.bfloat16)
        total = total + jnp.dot(terms, place, preferred_element_type=jnp.float32)
    lse_rows[...] = total
    lse_copy = pltpu.make_async_copy(lse_rows, lse, lse_store)
    lse_copy.start()
    for n in range(PLACES):
        load_part(n).wait()
        for which in range(2):
            lines, result, copy = store_part(n, which)
            for head in range(KV_HEADS):
                cols = slice(head * GROUP * HEAD_DIM, (head + 1) * GROUP * HEAD_DIM)
                block = held[head, :, 4 * n + 2 * which:4 * n + 2 * which + 2]
                result[lines, cols] = block.reshape(16, GROUP * HEAD_DIM)
            copy.start()
    for n in range(PLACES):
        for which in range(2):
            store_part(n, which)[2].wait()
    lse_copy.wait()


def local(queries, key_rows, value_rows, out_grad, doc_lengths, served_positions):
    bf16 = jnp.bfloat16
    dma = pltpu.SemaphoreType.DMA
    hbm = pl.BlockSpec(memory_space=pltpu.HBM)
    wide = HEADS * HEAD_DIM
    thin = KV_HEADS * HEAD_DIM
    result = pl.pallas_call(
        kernel,
        out_shape=jax.ShapeDtypeStruct((KV_HEADS, NY, TILES, GROUP, HEAD_DIM), bf16),
        in_specs=[hbm] * 6,
        out_specs=hbm,
        scratch_shapes=[
            pltpu.VMEM((NZ * 16, wide), bf16),
            pltpu.VMEM((NZ * 16, wide), bf16),
            pltpu.VMEM((128, thin), bf16),
            pltpu.VMEM((128, thin), bf16),
            pltpu.VMEM((SUBS, 8), jnp.int32),
            pltpu.VMEM((SUBS, HALF), jnp.int32),
            pltpu.VMEM((SLOTS, PLACES, 2, SUBS, GROUP, HEAD_DIM), bf16),
            pltpu.VMEM((KV_HEADS, KV_ROWS, HEAD_DIM), bf16),
            pltpu.VMEM((2, 16, 128), bf16),
            pltpu.VMEM((NCTX, 16, 128), bf16),
            pltpu.VMEM((NZ, 16, 128), bf16),
            pltpu.VMEM((NZ * SUBS, 2, SLOTS * GROUP, 128), jnp.float32),
            pltpu.VMEM((NZ, NCTX, KV_ROWS, HEAD_DIM), bf16),
            pltpu.VMEM((SLOTS, PLACES, 2, SUBS, GROUP, HEAD_DIM), bf16),
            pltpu.VMEM((SLOTS, TILES, GROUP, HEAD_DIM), bf16),
            pltpu.VMEM((SLOTS * GROUP, 128), jnp.float32),
            pltpu.SemaphoreType.REGULAR,
            dma((2, NZ)), dma((4,)), dma((2,)), dma((2,)), dma, dma, dma((NX,)),
            dma((2, 4)), dma((2, 4, NX)), dma, dma, dma, dma, dma, dma, dma,
        ],
        compiler_params=pltpu.CompilerParams(
            collective_id=0, has_side_effects=True, vmem_limit_bytes=VMEM_BYTES
        ),
        cost_estimate=pl.CostEstimate(flops=4 * 10**9, bytes_accessed=8 * 2**20,
                                      transcendentals=2 * 2**20),
    )(queries, out_grad, key_rows, value_rows, doc_lengths,
      served_positions.reshape(NZ * NY, SUBS).T)

    attended, lse, grad = pl.pallas_call(
        order_results,
        out_shape=(
            jax.ShapeDtypeStruct((NZ * 16, wide), bf16),
            jax.ShapeDtypeStruct((HEADS, 128), jnp.float32),
            jax.ShapeDtypeStruct((NZ * 16, wide), bf16),
        ),
        in_specs=[hbm],
        out_specs=(hbm, hbm, hbm),
        scratch_shapes=[
            pltpu.VMEM((KV_HEADS, NY, TILES, GROUP, HEAD_DIM), bf16),
            pltpu.VMEM((NZ * 16, wide), bf16),
            pltpu.VMEM((HEADS, 128), jnp.float32),
            pltpu.VMEM((NZ * 16, wide), bf16),
            dma((PLACES + 1,)), dma((2, PLACES)), dma,
        ],
        compiler_params=pltpu.CompilerParams(vmem_limit_bytes=VMEM_BYTES),
        cost_estimate=pl.CostEstimate(flops=0, bytes_accessed=4 * 2**20, transcendentals=0),
    )(result)
    return attended, lse.T, grad


def solution(mesh):
    in_specs = (
        P(("dp", "ctx"), None),
        P(("dp", "ctx"), None),
        P(("dp", "ctx"), None),
        P(("dp", "ctx"), None),
        P("dp", None),
        P("dp", "ctx", None, None),
    )
    out_specs = (P(("dp", "ctx"), None), P(("dp", "ctx"), None), P(("dp", "ctx"), None))
    return jax.shard_map(local, mesh=mesh, in_specs=in_specs, out_specs=out_specs, check_vma=False)
```

```python
import functools
import math

import jax
import jax.numpy as jnp
from jax import lax
from jax.experimental import pallas as pl
from jax.experimental.pallas import tpu as pltpu
from jax.sharding import PartitionSpec as P

HEAD_DIM = 128
HEADS = 32
KV_HEADS = 4
GROUP = HEADS // KV_HEADS
SUBS = 2
NZ = 8
NY = 8
NX = 4
NCTX = 8
SLOTS = 32
HALF = 64
SEQ = 512
PLACES = NY
TILES = 4 * PLACES + 1
EARLY = 3
STEPS = (0, 1, 3, 2)
KV_ROWS = 256
NEG_FILL = -1e30
VMEM_BYTES = 63 * 1024 * 1024
MESH = pl.DeviceIdType.MESH


def y_step(e, core):
    return e - 1 - 4 * core * (e // 3)


def rank(distance):
    return jnp.where(distance <= 4, jnp.maximum(2 * distance - 1, 0), 16 - 2 * distance)


def kernel(queries, grads, keys, values, lengths, positions, out,
           query_in, grad_in, key_in, value_in, lengths_in, positions_in,
           rows, kv_out, marks_out, marks_in, marks, bounds, kv, got, res, lse, second,
           load, small_load, row_send, row_recv, kva_send, kvb_send, kv_recv, ring_send, ring_recv,
           marka_send, markb_send, mark_recv, marks_send, marks_recv, res_send, res_recv):
    dp = lax.axis_index("dp")
    ctx = lax.axis_index("ctx")
    z, y = lax.div(dp, NY), lax.rem(dp, NY)
    x, core = lax.div(ctx, 2), lax.rem(ctx, 2)
    right = lax.rem(z + 1, NZ) * NY + y
    left = lax.rem(z + NZ - 1, NZ) * NY + y

    def at_y(step):
        return lax.rem(y + step + NY, NY)

    def at_ctx(x_step, core_step):
        return lax.rem(x + x_step, NX) * 2 + lax.rem(core + core_step, 2)

    def load_small(i):
        source, target = ((keys, key_in), (values, value_in), (lengths, lengths_in),
                          (positions, positions_in))[i]
        return pltpu.make_async_copy(source, target, small_load.at[i])

    for i in range(4):
        load_small(i).start()

    barrier = pltpu.get_barrier_semaphore()
    line = [(z * NY + at_y(step), ctx) for step in (1, -1, 2, -2)]
    near = [(dp, at_ctx(x_step, core_step)) for x_step in range(NX) for core_step in range(2)
            if x_step or core_step]
    far = z * NY + at_y(4)
    opposite = [(far, at_ctx(x_step, core_step)) for x_step in range(NX) for core_step in range(2)]
    ring_line = [(lax.rem(z + step, NZ) * NY + y, ctx) for step in range(1, NZ)]
    first_round = near + opposite + line + ring_line
    for dev in first_round:
        pl.semaphore_signal(barrier, inc=1, device_id=dev, device_id_type=MESH)

    def load_rows(home_z, which):
        block = pl.ds(home_z * 16, 16)
        source, target = ((queries, query_in), (grads, grad_in))[which]
        return pltpu.make_async_copy(source.at[block], target.at[block], load.at[which, home_z])

    for home_z in range(NZ):
        for which in range(2):
            load_rows(home_z, which).start()

    def order_rows(home_z, carry):
        place = rank(lax.rem(home_z - z + NZ, NZ))
        lines = pl.ds(pl.multiple_of(home_z * 16, 16), 16)
        for which, source in enumerate((query_in, grad_in)):
            load_rows(home_z, which).wait()
            for head in range(KV_HEADS):
                block = source[lines, head * GROUP * HEAD_DIM:(head + 1) * GROUP * HEAD_DIM]
                block = block.reshape(16, GROUP, HEAD_DIM)
                for home_y in range(NY):
                    rows[head * NY + home_y, place, which] = block[2 * home_y:2 * home_y + 2]
        return carry

    def remote(src, dst, send, recv, dev):
        return pltpu.make_async_remote_copy(src_ref=src, dst_ref=dst, send_sem=send, recv_sem=recv,
                                            device_id=dev, device_id_type=MESH)

    def wait_bytes(ref, sem):
        pltpu.make_async_copy(ref, ref, sem).wait()

    load_small(0).wait()
    load_small(1).wait()
    for head in range(KV_HEADS):
        cols = slice(head * HEAD_DIM, (head + 1) * HEAD_DIM)
        kv_out[head, 0:128] = key_in[:, cols]
        kv_out[head, 128:256] = value_in[:, cols]

    pl.semaphore_wait(barrier, len(first_round))
    for dev in line:
        pl.semaphore_signal(second, inc=1, device_id=dev, device_id_type=MESH)

    here = kv.at[z, ctx]
    arrived = kv_recv.at[x]

    @pl.when(core == 0)
    def _():
        pltpu.make_async_copy(kv_out.at[x], here, arrived).start()

    @pl.when(core != 0)
    def _():
        remote(kv_out.at[x], here, kva_send, arrived, (dp, x * 2)).start()

    remote(kv_out.at[x], here, kvb_send, arrived, (far, x * 2 + 1)).start()
    for x_step in STEPS[1:]:
        head = lax.rem(x + x_step, NX)
        remote(kv_out.at[head], here, kva_send, arrived, (dp, head * 2)).start()
        remote(kv_out.at[head], here, kvb_send, arrived, (far, head * 2 + 1)).start()

    load_small(2).wait()
    load_small(3).wait()
    pos = positions_in[...]
    spans = lengths_in[...]
    doc_lane = lax.broadcasted_iota(jnp.int32, (SUBS, 8), 1)
    first = jnp.zeros_like(pos)
    for doc in range(8):
        end = jnp.sum(jnp.where(doc_lane <= doc, spans, 0), axis=1, keepdims=True)
        first = jnp.where(pos >= end, end, first)
    spot = lax.broadcasted_iota(jnp.int32, (8, HALF), 0)
    table = jnp.zeros((8, HALF), jnp.int32)
    for s in range(SUBS):
        for part, line_value in enumerate((pos[s:s + 1, :], first[s:s + 1, :])):
            high = lax.shift_right_logical(line_value, 4)
            table = jnp.where(spot == s * 4 + part * 2, high, table)
            table = jnp.where(spot == s * 4 + part * 2 + 1, line_value - high * 16, table)
    table = table.astype(jnp.float32).astype(jnp.bfloat16)
    lane8 = lax.broadcasted_iota(jnp.int32, (8, 128), 1)
    row8 = lax.broadcasted_iota(jnp.int32, (8, 128), 0)
    lane64 = lax.broadcasted_iota(jnp.int32, (HALF, 128), 1)
    row64 = lax.broadcasted_iota(jnp.int32, (HALF, 128), 0)
    wanted = lax.rem(lax.div(lane8, 32), 2) * 4 + lax.rem(lane8, 4)

    for copy in range(2):
        made = []
        for e_hi in range(2):
            low, high = [at_y(4 * copy + y_step(2 * e_hi + e_lo, core)) for e_lo in range(2)]
            source = jnp.where(lane64 < 64, low, high) + lax.rem(lax.div(lane64, 4), NZ) * NY
            pick_rows = (row64 == source).astype(jnp.float32).astype(jnp.bfloat16)
            found = jnp.dot(table, pick_rows, preferred_element_type=jnp.float32)
            found = jnp.sum(jnp.where(row8 == wanted, found, 0.0), axis=0, keepdims=True)
            made.append(jnp.broadcast_to(found, (GROUP, 128)))
        made = jnp.concatenate(made, axis=0).astype(jnp.bfloat16)
        marks_out[copy] = made
    marks_here = marks_in.at[ctx]

    @pl.when(core == 0)
    def _():
        pltpu.make_async_copy(marks_out.at[0], marks_here, mark_recv).start()

    @pl.when(core != 0)
    def _():
        remote(marks_out.at[0], marks_here, marka_send, mark_recv, (dp, x * 2)).start()

    remote(marks_out.at[1], marks_here, markb_send, mark_recv, (far, x * 2 + 1)).start()
    for x_step in STEPS[1:]:
        head = lax.rem(x + x_step, NX)
        remote(marks_out.at[0], marks_here, marka_send, mark_recv, (dp, head * 2)).start()
        remote(marks_out.at[1], marks_here, markb_send, mark_recv, (far, head * 2 + 1)).start()

    def send_rows(part, which_e):
        ranks = pl.ds(0, EARLY) if part == 0 else pl.ds(EARLY, PLACES - EARLY)
        for e in which_e:
            server_y = at_y(-y_step(e, core))
            for other in range(2):
                copy = lax.rem(core + other, 2)
                home = lax.rem(server_y + 4 * copy, NY)
                for x_step in (1, 3, 2, 0):
                    head = lax.rem(x + x_step, NX)
                    src = rows.at[head * NY + home, ranks]
                    dst = got.at[(e % 2) * 16 + ctx * 2 + e // 2, ranks]
                    if e == 1 and other == 0 and x_step == 0:
                        pltpu.make_async_copy(src, dst, row_recv.at[part]).start()
                    else:
                        remote(src, dst, row_send.at[part], row_recv.at[part],
                               (z * NY + server_y, head * 2 + copy)).start()

    def piece(chunk, i):
        return kv.at[chunk, pl.ds(lax.rem(x + STEPS[i], NX) * 2, 2)]

    def from_left(step):
        return lax.rem(z - step + NZ, NZ)

    def from_right(step):
        return lax.rem(z + step, NZ)

    def pieces(step, way):
        return range(NX) if step < 3 else range(2 * way, 2 * way + 2)

    def forward(step, i):
        if i in pieces(step, 0):
            block = piece(from_left(step), i)
            remote(block, block, ring_send.at[0, step], ring_recv.at[0, step, i], (right, ctx)).start()
        if i in pieces(step, 1):
            block = piece(from_right(step), i)
            remote(block, block, ring_send.at[1, step], ring_recv.at[1, step, i], (left, ctx)).start()

    def begin_ring(i):
        wait_bytes(piece(z, i), kv_recv.at[lax.rem(x + STEPS[i], NX)])
        forward(0, i)

    def pass_on(step, which=range(NX)):
        for i in which:
            if i in pieces(step, 0):
                wait_bytes(piece(from_left(step + 1), i), ring_recv.at[0, step, i])
            if i in pieces(step, 1):
                wait_bytes(piece(from_right(step + 1), i), ring_recv.at[1, step, i])
            if step < 3:
                forward(step + 1, i)

    def begin_on(which_core, which):
        @pl.when(core == which_core)
        def _():
            for i in which:
                begin_ring(i)

    begin_on(0, range(NX))
    lax.fori_loop(0, NZ, order_rows, 0)
    pl.semaphore_wait(second, len(line))
    begin_on(1, (0,))
    send_rows(0, (0, 2, 3, 1))

    row16 = lax.broadcasted_iota(jnp.int32, (16, 128), 0)
    col16 = lax.broadcasted_iota(jnp.int32, (16, 128), 1)
    wait_bytes(marks_in, mark_recv)
    thin = (col16 == row16 * GROUP).astype(jnp.float32).astype(jnp.bfloat16)
    marks[z] = jnp.dot(thin, marks_in[...].reshape(128, 128),
                       preferred_element_type=jnp.float32).astype(jnp.bfloat16)
    for dev in ring_line:
        remote(marks.at[z], marks.at[z], marks_send, marks_recv, dev).start()
    begin_on(1, (1, 2))
    send_rows(1, (0, 2))
    begin_on(1, (3,))
    send_rows(1, (3, 1))

    scale = 1.0 / math.sqrt(HEAD_DIM)
    to_log2 = scale * math.log2(math.e)
    lane = lax.broadcasted_iota(jnp.int32, (128, 128), 0)
    key_pos = lax.broadcasted_iota(jnp.int32, (256, SEQ), 1).astype(jnp.float32)
    lse_lane = lax.broadcasted_iota(jnp.int32, (256, 128), 1)
    server_home = at_y(4 * core)

    def pick(base):
        return jnp.where(lane == base, 16.0, jnp.where(lane == base + 1, 1.0, 0.0)).astype(jnp.bfloat16)

    def dot(a, b, dims):
        return lax.dot_general(a, b, (dims, ((), ())), preferred_element_type=jnp.float32)

    row128 = lax.broadcasted_iota(jnp.int32, (128, 16), 0)
    col128 = lax.broadcasted_iota(jnp.int32, (128, 16), 1)
    widen = (lax.div(row128, GROUP) == col128).astype(jnp.float32).astype(jnp.bfloat16)

    def make_bounds(chunk, carry):
        wide = jnp.dot(widen, marks[chunk], preferred_element_type=jnp.float32).astype(jnp.bfloat16)
        for s in range(SUBS):
            for which in range(2):
                for e_lo in range(2):
                    base = e_lo * 64 + s * 32 + z * 4 + which * 2
                    bounds[chunk * SUBS + s, which, e_lo * 128:(e_lo + 1) * 128] = dot(
                        wide, pick(base), ((1,), (0,)))
        return carry

    def one_sequence(n, chunk, s):
        q = got[:, n, 0, s].reshape(256, HEAD_DIM)
        g = got[:, n, 1, s].reshape(256, HEAD_DIM)
        k = kv[chunk, :, pl.ds(pl.multiple_of(s * HALF, HALF), HALF), :].reshape(SEQ, HEAD_DIM)
        v = kv[chunk, :, pl.ds(pl.multiple_of(128 + s * HALF, HALF), HALF), :].reshape(SEQ, HEAD_DIM)
        last, first = [jnp.concatenate([bounds[chunk * SUBS + s, which]] * 4, axis=1)
                       for which in range(2)]
        visible = jnp.logical_and(key_pos <= last, key_pos >= first)
        scores = jnp.where(visible, dot(q, k, ((1,), (1,))) * to_log2, NEG_FILL)
        top = jnp.max(scores, axis=1, keepdims=True)
        p = jnp.exp2(scores - top)
        total = jnp.sum(p, axis=1, keepdims=True)
        inverse = 1.0 / total
        att = (dot(p.astype(jnp.bfloat16), v, ((1,), (0,))) * inverse).astype(jnp.bfloat16)
        delta = jnp.sum(g.astype(jnp.float32) * att.astype(jnp.float32), axis=1, keepdims=True)
        grad = dot(g, v, ((1,), (1,)))
        ds = (p * (grad - delta)).astype(jnp.bfloat16)
        dq = (dot(ds, k, ((1,), (0,))) * (inverse * scale)).astype(jnp.bfloat16)
        res[:, n * 4 + s] = att.reshape(SLOTS, GROUP, HEAD_DIM)
        res[:, n * 4 + 2 + s] = dq.reshape(SLOTS, GROUP, HEAD_DIM)
        left_over = (top + jnp.log2(total)) * math.log(2.0)
        kept = lse[...]
        for part in range(3):
            term = left_over.astype(jnp.bfloat16).astype(jnp.float32)
            left_over = left_over - term
            kept = jnp.where(lse_lane == part * 16 + chunk * SUBS + s, term, kept)
        lse[...] = kept

    def give(tiles):
        dst = out.at[x, server_home, tiles]
        for e in (0, 2, 3, 1):
            for other in range(2):
                home_core = lax.rem(core + other, 2)
                home_y = at_y(y_step(e, home_core))
                for x_step in (1, 3, 2, 0):
                    home_ctx = lax.rem(x + x_step, NX) * 2 + home_core
                    src = res.at[(e % 2) * 16 + home_ctx * 2 + e // 2, tiles]
                    if e == 1 and other == 0 and x_step == 0:
                        pltpu.make_async_copy(src, dst, res_recv).start()
                    else:
                        remote(src, dst, res_send, res_recv, (z * NY + home_y, home_ctx)).start()

    def rest_of_rows():
        wait_bytes(got.at[:, pl.ds(EARLY, PLACES - EARLY)], row_recv.at[1])

    def before(n):
        if n == 0:
            wait_bytes(got.at[:, pl.ds(0, EARLY)], row_recv.at[0])
        elif n == 1:
            pass_on(1, (0,))
        elif n == 2:
            pass_on(1, (1,))
        elif n == 3:
            pass_on(1, (2, 3))
            pass_on(2, (0,))
            rest_of_rows()
        elif n == 4:
            pass_on(2, (1,))
        elif n == 5:
            pass_on(2, (2, 3))
        elif n == 7:
            pass_on(3)

    def serve(n, carry):
        for turn in (0, 1, 2, 3, 4, 5, 7):
            pl.when(n == turn)(functools.partial(before, turn))
        chunk = lax.rem(z + lax.div(n + 1, 2) * (2 * lax.rem(n, 2) - 1) + NZ, NZ)

        def sub(s, inner):
            one_sequence(n, chunk, s)
            return inner

        lax.fori_loop(0, SUBS, sub, 0)
        give(pl.ds(n * 4, 4))
        return carry

    lse[...] = jnp.zeros_like(lse)
    pass_on(0)
    wait_bytes(marks.at[pl.ds(0, NZ - 1)], marks_recv)
    lax.fori_loop(0, NZ, make_bounds, 0)
    lax.fori_loop(0, PLACES, serve, 0)
    res[:, 4 * PLACES] = lse[...].astype(jnp.bfloat16).reshape(SLOTS, GROUP, 128)
    give(pl.ds(4 * PLACES, 1))

    sent = pl.ds(0, SLOTS - 1)
    wait_bytes(rows.at[sent, pl.ds(0, EARLY)], row_send.at[0])
    wait_bytes(rows.at[sent, pl.ds(EARLY, PLACES - EARLY)], row_send.at[1])
    wait_bytes(kv.at[0, pl.ds(0, 4)], kvb_send)
    wait_bytes(marks_in.at[pl.ds(0, 4)], markb_send)
    wait_bytes(marks.at[pl.ds(0, NZ - 1)], marks_send)

    @pl.when(core == 0)
    def _():
        wait_bytes(kv.at[0, pl.ds(0, 3)], kva_send)
        wait_bytes(marks_in.at[pl.ds(0, 3)], marka_send)

    @pl.when(core != 0)
    def _():
        wait_bytes(kv.at[0, pl.ds(0, 4)], kva_send)
        wait_bytes(marks_in.at[pl.ds(0, 4)], marka_send)

    for step in range(4):
        for way in range(2):
            wait_bytes(kv.at[0] if step < 3 else kv.at[0, pl.ds(0, 4)], ring_send.at[way, step])
    wait_bytes(res.at[sent], res_send)
    wait_bytes(out, res_recv)


def order_results(got, attended, lse, grad, held, attended_rows, lse_rows, grad_rows,
                  load, store, lse_store):
    z = lax.div(lax.axis_index("dp"), NY)

    def load_part(n):
        tiles = pl.ds(4 * n, 4) if n < PLACES else pl.ds(4 * PLACES, 1)
        return pltpu.make_async_copy(got.at[:, :, tiles], held.at[:, :, tiles], load.at[n])

    def store_part(n, which):
        chunk = lax.rem(z + ((n + 1) // 2) * (2 * (n % 2) - 1) + NZ, NZ)
        lines = pl.ds(pl.multiple_of(chunk * 16, 16), 16)
        source, target = ((attended_rows, attended), (grad_rows, grad))[which]
        return lines, source, pltpu.make_async_copy(source.at[lines], target.at[lines], store.at[which, n])

    order = [PLACES] + list(range(PLACES))
    for n in order:
        load_part(n).start()
    load_part(PLACES).wait()
    column = lax.broadcasted_iota(jnp.int32, (128, 128), 1)
    source = lax.broadcasted_iota(jnp.int32, (128, 128), 0)
    target = lax.div(lax.rem(source, 16), 2) * 16 + lax.rem(source, 2)
    target = jnp.where(source < 48, target, -128)
    total = jnp.zeros((HEADS, 128), jnp.float32)
    for home_y in range(NY):
        terms = held[:, home_y, 4 * PLACES].reshape(HEADS, 128)
        place = (column == target + home_y * SUBS).astype(jnp.float32).astype(jnp.bfloat16)
        total = total + jnp.dot(terms, place, preferred_element_type=jnp.float32)
    lse_rows[...] = total
    lse_copy = pltpu.make_async_copy(lse_rows, lse, lse_store)
    lse_copy.start()
    for n in range(PLACES):
        load_part(n).wait()
        for which in range(2):
            lines, result, copy = store_part(n, which)
            for head in range(KV_HEADS):
                cols = slice(head * GROUP * HEAD_DIM, (head + 1) * GROUP * HEAD_DIM)
                block = held[head, :, 4 * n + 2 * which:4 * n + 2 * which + 2]
                result[lines, cols] = block.reshape(16, GROUP * HEAD_DIM)
            copy.start()
    for n in range(PLACES):
        for which in range(2):
            store_part(n, which)[2].wait()
    lse_copy.wait()


def local(queries, key_rows, value_rows, out_grad, doc_lengths, served_positions):
    bf16 = jnp.bfloat16
    dma = pltpu.SemaphoreType.DMA
    hbm = pl.BlockSpec(memory_space=pltpu.HBM)
    wide = HEADS * HEAD_DIM
    thin = KV_HEADS * HEAD_DIM
    result = pl.pallas_call(
        kernel,
        out_shape=jax.ShapeDtypeStruct((KV_HEADS, NY, TILES, GROUP, HEAD_DIM), bf16),
        in_specs=[hbm] * 6,
        out_specs=hbm,
        scratch_shapes=[
            pltpu.VMEM((NZ * 16, wide), bf16),
            pltpu.VMEM((NZ * 16, wide), bf16),
            pltpu.VMEM((128, thin), bf16),
            pltpu.VMEM((128, thin), bf16),
            pltpu.VMEM((SUBS, 8), jnp.int32),
            pltpu.VMEM((SUBS, HALF), jnp.int32),
            pltpu.VMEM((SLOTS, PLACES, 2, SUBS, GROUP, HEAD_DIM), bf16),
            pltpu.VMEM((KV_HEADS, KV_ROWS, HEAD_DIM), bf16),
            pltpu.VMEM((2, 16, 128), bf16),
            pltpu.VMEM((NCTX, 16, 128), bf16),
            pltpu.VMEM((NZ, 16, 128), bf16),
            pltpu.VMEM((NZ * SUBS, 2, SLOTS * GROUP, 128), jnp.float32),
            pltpu.VMEM((NZ, NCTX, KV_ROWS, HEAD_DIM), bf16),
            pltpu.VMEM((SLOTS, PLACES, 2, SUBS, GROUP, HEAD_DIM), bf16),
            pltpu.VMEM((SLOTS, TILES, GROUP, HEAD_DIM), bf16),
            pltpu.VMEM((SLOTS * GROUP, 128), jnp.float32),
            pltpu.SemaphoreType.REGULAR,
            dma((2, NZ)), dma((4,)), dma((2,)), dma((2,)), dma, dma, dma((NX,)),
            dma((2, 4)), dma((2, 4, NX)), dma, dma, dma, dma, dma, dma, dma,
        ],
        compiler_params=pltpu.CompilerParams(
            collective_id=0, has_side_effects=True, vmem_limit_bytes=VMEM_BYTES
        ),
        cost_estimate=pl.CostEstimate(flops=4 * 10**9, bytes_accessed=8 * 2**20,
                                      transcendentals=2 * 2**20),
    )(queries, out_grad, key_rows, value_rows, doc_lengths,
      served_positions.reshape(NZ * NY, SUBS).T)

    attended, lse, grad = pl.pallas_call(
        order_results,
        out_shape=(
            jax.ShapeDtypeStruct((NZ * 16, wide), bf16),
            jax.ShapeDtypeStruct((HEADS, 128), jnp.float32),
            jax.ShapeDtypeStruct((NZ * 16, wide), bf16),
        ),
        in_specs=[hbm],
        out_specs=(hbm, hbm, hbm),
        scratch_shapes=[
            pltpu.VMEM((KV_HEADS, NY, TILES, GROUP, HEAD_DIM), bf16),
            pltpu.VMEM((NZ * 16, wide), bf16),
            pltpu.VMEM((HEADS, 128), jnp.float32),
            pltpu.VMEM((NZ * 16, wide), bf16),
            dma((PLACES + 1,)), dma((2, PLACES)), dma,
        ],
        compiler_params=pltpu.CompilerParams(vmem_limit_bytes=VMEM_BYTES),
        cost_estimate=pl.CostEstimate(flops=0, bytes_accessed=4 * 2**20, transcendentals=0),
    )(result)
    return attended, lse.T, grad


def solution(mesh):
    in_specs = (
        P(("dp", "ctx"), None),
        P(("dp", "ctx"), None),
        P(("dp", "ctx"), None),
        P(("dp", "ctx"), None),
        P("dp", None),
        P("dp", "ctx", None, None),
    )
    out_specs = (P(("dp", "ctx"), None), P(("dp", "ctx"), None), P(("dp", "ctx"), None))
    return jax.shard_map(local, mesh=mesh, in_specs=in_specs, out_specs=out_specs, check_vma=False)
```

```python
import functools
import math

import jax
import jax.numpy as jnp
from jax import lax
from jax.experimental import pallas as pl
from jax.experimental.pallas import tpu as pltpu
from jax.sharding import PartitionSpec as P

HEAD_DIM = 128
HEADS = 32
KV_HEADS = 4
GROUP = HEADS // KV_HEADS
SUBS = 2
NZ = 8
NY = 8
NX = 4
NCTX = 8
SLOTS = 32
HALF = 64
SEQ = 512
PLACES = NY
TILES = 4 * PLACES + SUBS
EARLY = 3
STEPS = (0, 1, 3, 2)
KV_ROWS = 256
NEG_FILL = -1e30
VMEM_BYTES = 63 * 1024 * 1024
MESH = pl.DeviceIdType.MESH


def y_step(e, copy, s):
    return e - 1 - 4 * (e // 3) * (copy if s else 1 - copy)


def away(copy, s):
    return (3 - 6 * s) * copy


def rank(distance):
    return jnp.where(distance <= 4, jnp.maximum(2 * distance - 1, 0), 16 - 2 * distance)


def kernel(queries, grads, keys, values, lengths, positions, out,
           query_in, grad_in, key_in, value_in, lengths_in, positions_in,
           rows, kv_out, marks_out, marks_in, marks, bounds, kv, got, res, lse, second,
           load, small_load, row_send, row_recv, kva_send, kvb_send, kv_recv, ring_send, ring_recv,
           marka_send, markb_send, mark_recv, marks_send, marks_recv, res_send, res_recv):
    dp = lax.axis_index("dp")
    ctx = lax.axis_index("ctx")
    z, y = lax.div(dp, NY), lax.rem(dp, NY)
    x, core = lax.div(ctx, 2), lax.rem(ctx, 2)
    right = lax.rem(z + 1, NZ) * NY + y
    left = lax.rem(z + NZ - 1, NZ) * NY + y

    def at_y(step):
        return lax.rem(y + step + NY, NY)

    def at_ctx(x_step, core_step):
        return lax.rem(x + x_step, NX) * 2 + lax.rem(core + core_step, 2)

    def load_small(i):
        source, target = ((keys, key_in), (values, value_in), (lengths, lengths_in),
                          (positions, positions_in))[i]
        return pltpu.make_async_copy(source, target, small_load.at[i])

    for i in range(4):
        load_small(i).start()

    barrier = pltpu.get_barrier_semaphore()
    line = [(z * NY + at_y(step), ctx) for step in (1, -1, 2, -2)]
    near = [(dp, at_ctx(x_step, core_step)) for x_step in range(NX) for core_step in range(2)
            if x_step or core_step]
    far = [z * NY + at_y(away(1, s)) for s in range(SUBS)]
    opposite = [(dev, at_ctx(x_step, core_step)) for dev in far for x_step in range(NX)
                for core_step in range(2)]
    ring_line = [(lax.rem(z + step, NZ) * NY + y, ctx) for step in range(1, NZ)]
    first_round = near + opposite + line + ring_line
    for dev in first_round:
        pl.semaphore_signal(barrier, inc=1, device_id=dev, device_id_type=MESH)

    def load_rows(home_z, which):
        block = pl.ds(home_z * 16, 16)
        source, target = ((queries, query_in), (grads, grad_in))[which]
        return pltpu.make_async_copy(source.at[block], target.at[block], load.at[which, home_z])

    for home_z in range(NZ):
        for which in range(2):
            load_rows(home_z, which).start()

    def order_rows(home_z, carry):
        place = rank(lax.rem(home_z - z + NZ, NZ))
        lines = pl.ds(pl.multiple_of(home_z * 16, 16), 16)
        for which, source in enumerate((query_in, grad_in)):
            load_rows(home_z, which).wait()
            for head in range(KV_HEADS):
                block = source[lines, head * GROUP * HEAD_DIM:(head + 1) * GROUP * HEAD_DIM]
                block = block.reshape(16, GROUP, HEAD_DIM)
                for home_y in range(NY):
                    for s in range(SUBS):
                        rows[head * NY + home_y, s, place, which] = block[2 * home_y + s]
        return carry

    def remote(src, dst, send, recv, dev):
        return pltpu.make_async_remote_copy(src_ref=src, dst_ref=dst, send_sem=send, recv_sem=recv,
                                            device_id=dev, device_id_type=MESH)

    def wait_bytes(ref, sem):
        pltpu.make_async_copy(ref, ref, sem).wait()

    load_small(0).wait()
    load_small(1).wait()
    for head in range(KV_HEADS):
        cols = slice(head * HEAD_DIM, (head + 1) * HEAD_DIM)
        for s in range(SUBS):
            kv_out[head, s * 128:s * 128 + HALF] = key_in[s * HALF:(s + 1) * HALF, cols]
            kv_out[head, s * 128 + HALF:(s + 1) * 128] = value_in[s * HALF:(s + 1) * HALF, cols]

    pl.semaphore_wait(barrier, len(first_round))
    for dev in line:
        pl.semaphore_signal(second, inc=1, device_id=dev, device_id_type=MESH)

    here = kv.at[z, ctx]
    arrived = kv_recv.at[x]

    @pl.when(core == 0)
    def _():
        pltpu.make_async_copy(kv_out.at[x], here, arrived).start()

    @pl.when(core != 0)
    def _():
        remote(kv_out.at[x], here, kva_send, arrived, (dp, x * 2)).start()

    def send_far(head):
        for s in range(SUBS):
            lines = pl.ds(s * 128, 128)
            remote(kv_out.at[head, lines], here.at[lines], kvb_send, arrived,
                   (far[s], head * 2 + 1)).start()

    send_far(x)
    for x_step in STEPS[1:]:
        head = lax.rem(x + x_step, NX)
        remote(kv_out.at[head], here, kva_send, arrived, (dp, head * 2)).start()
        send_far(head)

    load_small(2).wait()
    load_small(3).wait()
    pos = positions_in[...]
    spans = lengths_in[...]
    doc_lane = lax.broadcasted_iota(jnp.int32, (SUBS, 8), 1)
    first = jnp.zeros_like(pos)
    for doc in range(8):
        end = jnp.sum(jnp.where(doc_lane <= doc, spans, 0), axis=1, keepdims=True)
        first = jnp.where(pos >= end, end, first)
    spot = lax.broadcasted_iota(jnp.int32, (8, HALF), 0)
    table = jnp.zeros((8, HALF), jnp.int32)
    for s in range(SUBS):
        for part, line_value in enumerate((pos[s:s + 1, :], first[s:s + 1, :])):
            high = lax.shift_right_logical(line_value, 4)
            table = jnp.where(spot == s * 4 + part * 2, high, table)
            table = jnp.where(spot == s * 4 + part * 2 + 1, line_value - high * 16, table)
    table = table.astype(jnp.float32).astype(jnp.bfloat16)
    lane8 = lax.broadcasted_iota(jnp.int32, (8, 128), 1)
    row8 = lax.broadcasted_iota(jnp.int32, (8, 128), 0)
    lane64 = lax.broadcasted_iota(jnp.int32, (HALF, 128), 1)
    row64 = lax.broadcasted_iota(jnp.int32, (HALF, 128), 0)
    wanted = lax.rem(lax.div(lane8, 32), 2) * 4 + lax.rem(lane8, 4)

    for copy in range(2):
        made = []
        for e_hi in range(2):
            low, high = [
                jnp.where(lax.rem(lax.div(lane64, 32), 2) == 0,
                          *[at_y(away(copy, s) + y_step(2 * e_hi + e_lo, copy, s)) for s in range(SUBS)])
                for e_lo in range(2)]
            source = jnp.where(lane64 < 64, low, high) + lax.rem(lax.div(lane64, 4), NZ) * NY
            pick_rows = (row64 == source).astype(jnp.float32).astype(jnp.bfloat16)
            found = jnp.dot(table, pick_rows, preferred_element_type=jnp.float32)
            found = jnp.sum(jnp.where(row8 == wanted, found, 0.0), axis=0, keepdims=True)
            made.append(jnp.broadcast_to(found, (GROUP, 128)))
        made = jnp.concatenate(made, axis=0).astype(jnp.bfloat16)
        marks_out[copy] = made

    @pl.when(core == 0)
    def _():
        for s in range(SUBS):
            pltpu.make_async_copy(marks_out.at[0], marks_in.at[s, ctx], mark_recv).start()

    @pl.when(core != 0)
    def _():
        for s in range(SUBS):
            remote(marks_out.at[0], marks_in.at[s, ctx], marka_send, mark_recv, (dp, x * 2)).start()

    for x_step in STEPS:
        head = lax.rem(x + x_step, NX)
        for s in range(SUBS):
            if x_step:
                remote(marks_out.at[0], marks_in.at[s, ctx], marka_send, mark_recv, (dp, head * 2)).start()
            remote(marks_out.at[1], marks_in.at[s, ctx], markb_send, mark_recv,
                   (far[s], head * 2 + 1)).start()

    def send_rows(part, which_e):
        ranks = pl.ds(0, EARLY) if part == 0 else pl.ds(EARLY, PLACES - EARLY)
        for e in which_e:
            for other in range(2):
                copy = lax.rem(core + other, 2)
                for s in range(SUBS):
                    server_y = at_y(-y_step(e, copy, s))
                    home = lax.rem(server_y + NY - away(copy, s), NY)
                    for x_step in (1, 3, 2, 0):
                        head = lax.rem(x + x_step, NX)
                        src = rows.at[head * NY + home, s, ranks]
                        dst = got.at[(e % 2) * 16 + ctx * 2 + e // 2, s, ranks]
                        if e == 1 and other == 0 and x_step == 0:
                            pltpu.make_async_copy(src, dst, row_recv.at[part]).start()
                        else:
                            remote(src, dst, row_send.at[part], row_recv.at[part],
                                   (z * NY + server_y, head * 2 + copy)).start()

    def piece(chunk, i):
        return kv.at[chunk, pl.ds(lax.rem(x + STEPS[i], NX) * 2, 2)]

    def from_left(step):
        return lax.rem(z - step + NZ, NZ)

    def from_right(step):
        return lax.rem(z + step, NZ)

    def pieces(step, way):
        return range(NX) if step < 3 else range(2 * way, 2 * way + 2)

    def forward(step, i):
        if i in pieces(step, 0):
            block = piece(from_left(step), i)
            remote(block, block, ring_send.at[0, step], ring_recv.at[0, step, i], (right, ctx)).start()
        if i in pieces(step, 1):
            block = piece(from_right(step), i)
            remote(block, block, ring_send.at[1, step], ring_recv.at[1, step, i], (left, ctx)).start()

    def begin_ring(i):
        wait_bytes(piece(z, i), kv_recv.at[lax.rem(x + STEPS[i], NX)])
        forward(0, i)

    def pass_on(step, which=range(NX)):
        for i in which:
            if i in pieces(step, 0):
                wait_bytes(piece(from_left(step + 1), i), ring_recv.at[0, step, i])
            if i in pieces(step, 1):
                wait_bytes(piece(from_right(step + 1), i), ring_recv.at[1, step, i])
            if step < 3:
                forward(step + 1, i)

    def begin_on(which_core, which):
        @pl.when(core == which_core)
        def _():
            for i in which:
                begin_ring(i)

    begin_on(0, range(NX))
    lax.fori_loop(0, NZ, order_rows, 0)
    pl.semaphore_wait(second, len(line))
    begin_on(1, (0,))
    send_rows(0, (0, 2, 3, 1))

    row16 = lax.broadcasted_iota(jnp.int32, (16, 128), 0)
    col16 = lax.broadcasted_iota(jnp.int32, (16, 128), 1)
    wait_bytes(marks_in, mark_recv)
    thin = (col16 == row16 * GROUP).astype(jnp.float32).astype(jnp.bfloat16)
    found = [jnp.dot(thin, marks_in[s].reshape(128, 128), preferred_element_type=jnp.float32)
             for s in range(SUBS)]
    marks[z] = jnp.where(lax.rem(lax.div(col16, 32), 2) == 0, *found).astype(jnp.bfloat16)
    for dev in ring_line:
        remote(marks.at[z], marks.at[z], marks_send, marks_recv, dev).start()
    begin_on(1, (1, 2))
    send_rows(1, (0, 2))
    begin_on(1, (3,))
    send_rows(1, (3, 1))

    scale = 1.0 / math.sqrt(HEAD_DIM)
    to_log2 = scale * math.log2(math.e)
    lane = lax.broadcasted_iota(jnp.int32, (128, 128), 0)
    key_pos = lax.broadcasted_iota(jnp.int32, (256, SEQ), 1).astype(jnp.float32)
    lse_lane = lax.broadcasted_iota(jnp.int32, (256, 128), 1)
    server_home = [at_y(-away(core, s)) for s in range(SUBS)]

    def pick(base):
        return jnp.where(lane == base, 16.0, jnp.where(lane == base + 1, 1.0, 0.0)).astype(jnp.bfloat16)

    def dot(a, b, dims):
        return lax.dot_general(a, b, (dims, ((), ())), preferred_element_type=jnp.float32)

    row128 = lax.broadcasted_iota(jnp.int32, (128, 16), 0)
    col128 = lax.broadcasted_iota(jnp.int32, (128, 16), 1)
    widen = (lax.div(row128, GROUP) == col128).astype(jnp.float32).astype(jnp.bfloat16)

    def make_bounds(chunk, carry):
        wide = jnp.dot(widen, marks[chunk], preferred_element_type=jnp.float32).astype(jnp.bfloat16)
        for s in range(SUBS):
            for which in range(2):
                for e_lo in range(2):
                    base = e_lo * 64 + s * 32 + z * 4 + which * 2
                    bounds[chunk * SUBS + s, which, e_lo * 128:(e_lo + 1) * 128] = dot(
                        wide, pick(base), ((1,), (0,)))
        return carry

    def one_sequence(n, chunk, s):
        q = got[:, s, n, 0].reshape(256, HEAD_DIM)
        g = got[:, s, n, 1].reshape(256, HEAD_DIM)
        k = kv[chunk, :, pl.ds(pl.multiple_of(s * 128, 128), HALF), :].reshape(SEQ, HEAD_DIM)
        v = kv[chunk, :, pl.ds(pl.multiple_of(s * 128 + HALF, HALF), HALF), :].reshape(SEQ, HEAD_DIM)
        last, first = [jnp.concatenate([bounds[chunk * SUBS + s, which]] * 4, axis=1)
                       for which in range(2)]
        visible = jnp.logical_and(key_pos <= last, key_pos >= first)
        scores = jnp.where(visible, dot(q, k, ((1,), (1,))) * to_log2, NEG_FILL)
        top = jnp.max(scores, axis=1, keepdims=True)
        p = jnp.exp2(scores - top)
        total = jnp.sum(p, axis=1, keepdims=True)
        inverse = 1.0 / total
        att = (dot(p.astype(jnp.bfloat16), v, ((1,), (0,))) * inverse).astype(jnp.bfloat16)
        delta = jnp.sum(g.astype(jnp.float32) * att.astype(jnp.float32), axis=1, keepdims=True)
        grad = dot(g, v, ((1,), (1,)))
        ds = (p * (grad - delta)).astype(jnp.bfloat16)
        dq = (dot(ds, k, ((1,), (0,))) * (inverse * scale)).astype(jnp.bfloat16)
        res[:, n * 4 + 2 * s] = att.reshape(SLOTS, GROUP, HEAD_DIM)
        res[:, n * 4 + 2 * s + 1] = dq.reshape(SLOTS, GROUP, HEAD_DIM)
        left_over = (top + jnp.log2(total)) * math.log(2.0)
        kept = lse[...]
        for part in range(3):
            term = left_over.astype(jnp.bfloat16).astype(jnp.float32)
            left_over = left_over - term
            kept = jnp.where(lse_lane == part * 16 + chunk * SUBS + s, term, kept)
        lse[...] = kept

    def give(first_tile, count):
        for e in (0, 2, 3, 1):
            for s in range(SUBS):
                tiles = pl.ds(first_tile + s * count, count)
                dst = out.at[x, server_home[s], tiles]
                home_y = at_y(y_step(e, core, s))
                for other in range(2):
                    home_core = lax.rem(core + other, 2)
                    for x_step in (1, 3, 2, 0):
                        home_ctx = lax.rem(x + x_step, NX) * 2 + home_core
                        src = res.at[(e % 2) * 16 + home_ctx * 2 + e // 2, tiles]
                        if e == 1 and other == 0 and x_step == 0:
                            pltpu.make_async_copy(src, dst, res_recv).start()
                        else:
                            remote(src, dst, res_send, res_recv, (z * NY + home_y, home_ctx)).start()

    def rest_of_rows():
        wait_bytes(got.at[:, :, pl.ds(EARLY, PLACES - EARLY)], row_recv.at[1])

    def before(n):
        if n == 0:
            wait_bytes(got.at[:, :, pl.ds(0, EARLY)], row_recv.at[0])
        elif n == 1:
            pass_on(1, (0,))
        elif n == 2:
            pass_on(1, (1,))
        elif n == 3:
            pass_on(1, (2, 3))
            pass_on(2, (0,))
            rest_of_rows()
        elif n == 4:
            pass_on(2, (1,))
        elif n == 5:
            pass_on(2, (2, 3))
        elif n == 7:
            pass_on(3)

    def serve(n, carry):
        for turn in (0, 1, 2, 3, 4, 5, 7):
            pl.when(n == turn)(functools.partial(before, turn))
        chunk = lax.rem(z + lax.div(n + 1, 2) * (2 * lax.rem(n, 2) - 1) + NZ, NZ)

        def sub(s, inner):
            one_sequence(n, chunk, s)
            return inner

        lax.fori_loop(0, SUBS, sub, 0)
        give(n * 4, 2)
        return carry

    lse[...] = jnp.zeros_like(lse)
    pass_on(0)
    wait_bytes(marks.at[pl.ds(0, NZ - 1)], marks_recv)
    lax.fori_loop(0, NZ, make_bounds, 0)
    lax.fori_loop(0, PLACES, serve, 0)
    for s in range(SUBS):
        res[:, 4 * PLACES + s] = lse[...].astype(jnp.bfloat16).reshape(SLOTS, GROUP, 128)
    give(4 * PLACES, 1)

    sent = pl.ds(0, SLOTS - 1)
    wait_bytes(rows.at[sent, :, pl.ds(0, EARLY)], row_send.at[0])
    wait_bytes(rows.at[sent, :, pl.ds(EARLY, PLACES - EARLY)], row_send.at[1])
    wait_bytes(kv.at[0, pl.ds(0, 4)], kvb_send)
    wait_bytes(marks_in.at[0], markb_send)
    wait_bytes(marks.at[pl.ds(0, NZ - 1)], marks_send)

    @pl.when(core == 0)
    def _():
        wait_bytes(kv.at[0, pl.ds(0, 3)], kva_send)
        wait_bytes(marks_in.at[0, pl.ds(0, 6)], marka_send)

    @pl.when(core != 0)
    def _():
        wait_bytes(kv.at[0, pl.ds(0, 4)], kva_send)
        wait_bytes(marks_in.at[0], marka_send)

    for step in range(4):
        for way in range(2):
            wait_bytes(kv.at[0] if step < 3 else kv.at[0, pl.ds(0, 4)], ring_send.at[way, step])
    wait_bytes(res.at[sent], res_send)
    wait_bytes(out, res_recv)


def order_results(got, attended, lse, grad, held, attended_rows, lse_rows, grad_rows,
                  load, store, lse_store):
    z = lax.div(lax.axis_index("dp"), NY)

    def load_part(n):
        tiles = pl.ds(4 * n, 4) if n < PLACES else pl.ds(4 * PLACES, SUBS)
        return pltpu.make_async_copy(got.at[:, :, tiles], held.at[:, :, tiles], load.at[n])

    def store_part(n, which):
        chunk = lax.rem(z + ((n + 1) // 2) * (2 * (n % 2) - 1) + NZ, NZ)
        lines = pl.ds(pl.multiple_of(chunk * 16, 16), 16)
        source, target = ((attended_rows, attended), (grad_rows, grad))[which]
        return lines, source, pltpu.make_async_copy(source.at[lines], target.at[lines], store.at[which, n])

    order = [PLACES] + list(range(PLACES))
    for n in order:
        load_part(n).start()
    load_part(PLACES).wait()
    column = lax.broadcasted_iota(jnp.int32, (128, 128), 1)
    source = lax.broadcasted_iota(jnp.int32, (128, 128), 0)
    target = lax.div(lax.rem(source, 16), 2) * 16 + lax.rem(source, 2)
    target = jnp.where(source < 48, target, -128)
    total = jnp.zeros((HEADS, 128), jnp.float32)
    for home_y in range(NY):
        terms = [held[:, home_y, 4 * PLACES + s].reshape(HEADS, 128).astype(jnp.float32)
                 for s in range(SUBS)]
        terms = jnp.where(lax.rem(column[:HEADS], 2) == 0, *terms).astype(jnp.bfloat16)
        place = (column == target + home_y * SUBS).astype(jnp.float32).astype(jnp.bfloat16)
        total = total + jnp.dot(terms, place, preferred_element_type=jnp.float32)
    lse_rows[...] = total
    lse_copy = pltpu.make_async_copy(lse_rows, lse, lse_store)
    lse_copy.start()
    for n in range(PLACES):
        load_part(n).wait()
        for which in range(2):
            lines, result, copy = store_part(n, which)
            for head in range(KV_HEADS):
                cols = slice(head * GROUP * HEAD_DIM, (head + 1) * GROUP * HEAD_DIM)
                block = jnp.stack([held[head, :, 4 * n + 2 * s + which] for s in range(SUBS)], axis=1)
                result[lines, cols] = block.reshape(16, GROUP * HEAD_DIM)
            copy.start()
    for n in range(PLACES):
        for which in range(2):
            store_part(n, which)[2].wait()
    lse_copy.wait()


def local(queries, key_rows, value_rows, out_grad, doc_lengths, served_positions):
    bf16 = jnp.bfloat16
    dma = pltpu.SemaphoreType.DMA
    hbm = pl.BlockSpec(memory_space=pltpu.HBM)
    wide = HEADS * HEAD_DIM
    thin = KV_HEADS * HEAD_DIM
    result = pl.pallas_call(
        kernel,
        out_shape=jax.ShapeDtypeStruct((KV_HEADS, NY, TILES, GROUP, HEAD_DIM), bf16),
        in_specs=[hbm] * 6,
        out_specs=hbm,
        scratch_shapes=[
            pltpu.VMEM((NZ * 16, wide), bf16),
            pltpu.VMEM((NZ * 16, wide), bf16),
            pltpu.VMEM((128, thin), bf16),
            pltpu.VMEM((128, thin), bf16),
            pltpu.VMEM((SUBS, 8), jnp.int32),
            pltpu.VMEM((SUBS, HALF), jnp.int32),
            pltpu.VMEM((SLOTS, SUBS, PLACES, 2, GROUP, HEAD_DIM), bf16),
            pltpu.VMEM((KV_HEADS, KV_ROWS, HEAD_DIM), bf16),
            pltpu.VMEM((2, 16, 128), bf16),
            pltpu.VMEM((SUBS, NCTX, 16, 128), bf16),
            pltpu.VMEM((NZ, 16, 128), bf16),
            pltpu.VMEM((NZ * SUBS, 2, SLOTS * GROUP, 128), jnp.float32),
            pltpu.VMEM((NZ, NCTX, KV_ROWS, HEAD_DIM), bf16),
            pltpu.VMEM((SLOTS, SUBS, PLACES, 2, GROUP, HEAD_DIM), bf16),
            pltpu.VMEM((SLOTS, TILES, GROUP, HEAD_DIM), bf16),
            pltpu.VMEM((SLOTS * GROUP, 128), jnp.float32),
            pltpu.SemaphoreType.REGULAR,
            dma((2, NZ)), dma((4,)), dma((2,)), dma((2,)), dma, dma, dma((NX,)),
            dma((2, 4)), dma((2, 4, NX)), dma, dma, dma, dma, dma, dma, dma,
        ],
        compiler_params=pltpu.CompilerParams(
            collective_id=0, has_side_effects=True, vmem_limit_bytes=VMEM_BYTES
        ),
        cost_estimate=pl.CostEstimate(flops=4 * 10**9, bytes_accessed=8 * 2**20,
                                      transcendentals=2 * 2**20),
    )(queries, out_grad, key_rows, value_rows, doc_lengths,
      served_positions.reshape(NZ * NY, SUBS).T)

    attended, lse, grad = pl.pallas_call(
        order_results,
        out_shape=(
            jax.ShapeDtypeStruct((NZ * 16, wide), bf16),
            jax.ShapeDtypeStruct((HEADS, 128), jnp.float32),
            jax.ShapeDtypeStruct((NZ * 16, wide), bf16),
        ),
        in_specs=[hbm],
        out_specs=(hbm, hbm, hbm),
        scratch_shapes=[
            pltpu.VMEM((KV_HEADS, NY, TILES, GROUP, HEAD_DIM), bf16),
            pltpu.VMEM((NZ * 16, wide), bf16),
            pltpu.VMEM((HEADS, 128), jnp.float32),
            pltpu.VMEM((NZ * 16, wide), bf16),
            dma((PLACES + 1,)), dma((2, PLACES)), dma,
        ],
        compiler_params=pltpu.CompilerParams(vmem_limit_bytes=VMEM_BYTES),
        cost_estimate=pl.CostEstimate(flops=0, bytes_accessed=4 * 2**20, transcendentals=0),
    )(result)
    return attended, lse.T, grad


def solution(mesh):
    in_specs = (
        P(("dp", "ctx"), None),
        P(("dp", "ctx"), None),
        P(("dp", "ctx"), None),
        P(("dp", "ctx"), None),
        P("dp", None),
        P("dp", "ctx", None, None),
    )
    out_specs = (P(("dp", "ctx"), None), P(("dp", "ctx"), None), P(("dp", "ctx"), None))
    return jax.shard_map(local, mesh=mesh, in_specs=in_specs, out_specs=out_specs, check_vma=False)
```

```python
import functools
import math

import jax
import jax.numpy as jnp
from jax import lax
from jax.experimental import pallas as pl
from jax.experimental.pallas import tpu as pltpu
from jax.sharding import PartitionSpec as P

HEAD_DIM = 128
HEADS = 32
KV_HEADS = 4
GROUP = HEADS // KV_HEADS
SUBS = 2
NZ = 8
NY = 8
NX = 4
NCTX = 8
SLOTS = 32
HALF = 64
SEQ = 512
PLACES = NY
TILES = 4 * PLACES + SUBS
EARLY = 3
STEPS = (0, 1, 3, 2)
KV_ROWS = 256
NEG_FILL = -1e30
VMEM_BYTES = 63 * 1024 * 1024
MESH = pl.DeviceIdType.MESH


def y_step(e, copy, s):
    return e - 1 - 4 * (e // 3) * (copy if s else 1 - copy)


def away(copy, s):
    return (3 - 6 * s) * copy


def rank(distance):
    return jnp.where(distance <= 4, jnp.maximum(2 * distance - 1, 0), 16 - 2 * distance)


def kernel(queries, grads, keys, values, lengths, positions, out,
           query_in, grad_in, key_in, value_in, lengths_in, positions_in,
           rows, kv_out, marks_out, marks_in, marks, bounds, kv, got, res, lse, second,
           load, small_load, row_send, row_recv, kva_send, kvb_send, kv_recv, ring_send, ring_recv,
           marka_send, markb_send, mark_recv, marks_send, marks_recv, res_send, res_recv):
    dp = lax.axis_index("dp")
    ctx = lax.axis_index("ctx")
    z, y = lax.div(dp, NY), lax.rem(dp, NY)
    x, core = lax.div(ctx, 2), lax.rem(ctx, 2)
    right = lax.rem(z + 1, NZ) * NY + y
    left = lax.rem(z + NZ - 1, NZ) * NY + y

    def at_y(step):
        return lax.rem(y + step + NY, NY)

    def at_ctx(x_step, core_step):
        return lax.rem(x + x_step, NX) * 2 + lax.rem(core + core_step, 2)

    def load_small(i):
        source, target = ((keys, key_in), (values, value_in), (lengths, lengths_in),
                          (positions, positions_in))[i]
        return pltpu.make_async_copy(source, target, small_load.at[i])

    for i in range(4):
        load_small(i).start()

    barrier = pltpu.get_barrier_semaphore()
    line = [(z * NY + at_y(step), ctx) for step in (1, -1, 2, -2)]
    near = [(dp, at_ctx(x_step, core_step)) for x_step in range(NX) for core_step in range(2)
            if x_step or core_step]
    far = [z * NY + at_y(away(1, s)) for s in range(SUBS)]
    opposite = [(dev, at_ctx(x_step, core_step)) for dev in far for x_step in range(NX)
                for core_step in range(2)]
    ring_line = [(lax.rem(z + step, NZ) * NY + y, ctx) for step in range(1, NZ)]
    first_round = near + opposite + line + ring_line
    for dev in first_round:
        pl.semaphore_signal(barrier, inc=1, device_id=dev, device_id_type=MESH)

    def load_rows(home_z, which):
        block = pl.ds(home_z * 16, 16)
        source, target = ((queries, query_in), (grads, grad_in))[which]
        return pltpu.make_async_copy(source.at[block], target.at[block], load.at[which, home_z])

    for home_z in range(NZ):
        for which in range(2):
            load_rows(home_z, which).start()

    def order_rows(home_z, carry):
        place = rank(lax.rem(home_z - z + NZ, NZ))
        lines = pl.ds(pl.multiple_of(home_z * 16, 16), 16)
        for which, source in enumerate((query_in, grad_in)):
            load_rows(home_z, which).wait()
            for head in range(KV_HEADS):
                block = source[lines, head * GROUP * HEAD_DIM:(head + 1) * GROUP * HEAD_DIM]
                block = block.reshape(16, GROUP, HEAD_DIM)
                for home_y in range(NY):
                    for s in range(SUBS):
                        rows[head * NY + home_y, s, place, which] = block[2 * home_y + s]
        return carry

    def remote(src, dst, send, recv, dev):
        return pltpu.make_async_remote_copy(src_ref=src, dst_ref=dst, send_sem=send, recv_sem=recv,
                                            device_id=dev, device_id_type=MESH)

    def wait_bytes(ref, sem):
        pltpu.make_async_copy(ref, ref, sem).wait()

    load_small(0).wait()
    load_small(1).wait()
    for head in range(KV_HEADS):
        cols = slice(head * HEAD_DIM, (head + 1) * HEAD_DIM)
        for s in range(SUBS):
            kv_out[head, s * 128:s * 128 + HALF] = key_in[s * HALF:(s + 1) * HALF, cols]
            kv_out[head, s * 128 + HALF:(s + 1) * 128] = value_in[s * HALF:(s + 1) * HALF, cols]

    pl.semaphore_wait(barrier, len(first_round))
    for dev in line:
        pl.semaphore_signal(second, inc=1, device_id=dev, device_id_type=MESH)

    here = kv.at[z, ctx]
    arrived = kv_recv.at[x]

    @pl.when(core == 0)
    def _():
        pltpu.make_async_copy(kv_out.at[x], here, arrived).start()

    @pl.when(core != 0)
    def _():
        remote(kv_out.at[x], here, kva_send, arrived, (dp, x * 2)).start()

    def send_far(head):
        for s in range(SUBS):
            lines = pl.ds(s * 128, 128)
            remote(kv_out.at[head, lines], here.at[lines], kvb_send, arrived,
                   (far[s], head * 2 + 1)).start()

    send_far(x)
    for x_step in STEPS[1:]:
        head = lax.rem(x + x_step, NX)
        remote(kv_out.at[head], here, kva_send, arrived, (dp, head * 2)).start()
        send_far(head)

    load_small(2).wait()
    load_small(3).wait()
    pos = positions_in[...]
    spans = lengths_in[...]
    doc_lane = lax.broadcasted_iota(jnp.int32, (SUBS, 8), 1)
    first = jnp.zeros_like(pos)
    for doc in range(8):
        end = jnp.sum(jnp.where(doc_lane <= doc, spans, 0), axis=1, keepdims=True)
        first = jnp.where(pos >= end, end, first)
    spot = lax.broadcasted_iota(jnp.int32, (8, HALF), 0)
    table = jnp.zeros((8, HALF), jnp.int32)
    for s in range(SUBS):
        for part, line_value in enumerate((pos[s:s + 1, :], first[s:s + 1, :])):
            high = lax.shift_right_logical(line_value, 4)
            table = jnp.where(spot == s * 4 + part * 2, high, table)
            table = jnp.where(spot == s * 4 + part * 2 + 1, line_value - high * 16, table)
    table = table.astype(jnp.float32).astype(jnp.bfloat16)
    lane8 = lax.broadcasted_iota(jnp.int32, (8, 128), 1)
    row8 = lax.broadcasted_iota(jnp.int32, (8, 128), 0)
    lane64 = lax.broadcasted_iota(jnp.int32, (HALF, 128), 1)
    row64 = lax.broadcasted_iota(jnp.int32, (HALF, 128), 0)
    wanted = lax.rem(lax.div(lane8, 32), 2) * 4 + lax.rem(lane8, 4)

    for copy in range(2):
        made = []
        for e_hi in range(2):
            low, high = [
                jnp.where(lax.rem(lax.div(lane64, 32), 2) == 0,
                          *[at_y(away(copy, s) + y_step(2 * e_hi + e_lo, copy, s)) for s in range(SUBS)])
                for e_lo in range(2)]
            source = jnp.where(lane64 < 64, low, high) + lax.rem(lax.div(lane64, 4), NZ) * NY
            pick_rows = (row64 == source).astype(jnp.float32).astype(jnp.bfloat16)
            found = jnp.dot(table, pick_rows, preferred_element_type=jnp.float32)
            found = jnp.sum(jnp.where(row8 == wanted, found, 0.0), axis=0, keepdims=True)
            made.append(jnp.broadcast_to(found, (GROUP, 128)))
        made = jnp.concatenate(made, axis=0).astype(jnp.bfloat16)
        marks_out[copy] = made

    @pl.when(core == 0)
    def _():
        for s in range(SUBS):
            pltpu.make_async_copy(marks_out.at[0], marks_in.at[s, ctx], mark_recv).start()

    @pl.when(core != 0)
    def _():
        for s in range(SUBS):
            remote(marks_out.at[0], marks_in.at[s, ctx], marka_send, mark_recv, (dp, x * 2)).start()

    for x_step in STEPS:
        head = lax.rem(x + x_step, NX)
        for s in range(SUBS):
            if x_step:
                remote(marks_out.at[0], marks_in.at[s, ctx], marka_send, mark_recv, (dp, head * 2)).start()
            remote(marks_out.at[1], marks_in.at[s, ctx], markb_send, mark_recv,
                   (far[s], head * 2 + 1)).start()

    def send_rows(part, which_e):
        ranks = pl.ds(0, EARLY) if part == 0 else pl.ds(EARLY, PLACES - EARLY)
        for e in which_e:
            for other in range(2):
                copy = lax.rem(core + other, 2)
                for s in range(SUBS):
                    server_y = at_y(-y_step(e, copy, s))
                    home = lax.rem(server_y + NY - away(copy, s), NY)
                    for x_step in (1, 3, 2, 0):
                        head = lax.rem(x + x_step, NX)
                        src = rows.at[head * NY + home, s, ranks]
                        dst = got.at[(e % 2) * 16 + ctx * 2 + e // 2, s, ranks]
                        if e == 1 and other == 0 and x_step == 0:
                            pltpu.make_async_copy(src, dst, row_recv.at[part]).start()
                        else:
                            remote(src, dst, row_send.at[part], row_recv.at[part],
                                   (z * NY + server_y, head * 2 + copy)).start()

    def piece(chunk, i):
        return kv.at[chunk, pl.ds(lax.rem(x + STEPS[i], NX) * 2, 2)]

    def from_left(step):
        return lax.rem(z - step + NZ, NZ)

    def from_right(step):
        return lax.rem(z + step, NZ)

    def pieces(step, way):
        return range(NX) if step < 3 else range(2 * way, 2 * way + 2)

    def forward(step, i):
        if i in pieces(step, 0):
            block = piece(from_left(step), i)
            remote(block, block, ring_send.at[0, step], ring_recv.at[0, step, i], (right, ctx)).start()
        if i in pieces(step, 1):
            block = piece(from_right(step), i)
            remote(block, block, ring_send.at[1, step], ring_recv.at[1, step, i], (left, ctx)).start()

    def begin_ring(i):
        wait_bytes(piece(z, i), kv_recv.at[lax.rem(x + STEPS[i], NX)])
        forward(0, i)

    def pass_on(step, which=range(NX)):
        for i in which:
            if i in pieces(step, 0):
                wait_bytes(piece(from_left(step + 1), i), ring_recv.at[0, step, i])
            if i in pieces(step, 1):
                wait_bytes(piece(from_right(step + 1), i), ring_recv.at[1, step, i])
            if step < 3:
                forward(step + 1, i)

    def begin_on(which_core, which):
        @pl.when(core == which_core)
        def _():
            for i in which:
                begin_ring(i)

    begin_on(0, range(NX))
    lax.fori_loop(0, NZ, order_rows, 0)
    pl.semaphore_wait(second, len(line))
    begin_on(1, (0,))
    send_rows(0, (0, 2, 3, 1))

    row16 = lax.broadcasted_iota(jnp.int32, (16, 128), 0)
    col16 = lax.broadcasted_iota(jnp.int32, (16, 128), 1)
    wait_bytes(marks_in, mark_recv)
    thin = (col16 == row16 * GROUP).astype(jnp.float32).astype(jnp.bfloat16)
    found = [jnp.dot(thin, marks_in[s].reshape(128, 128), preferred_element_type=jnp.float32)
             for s in range(SUBS)]
    marks[z] = jnp.where(lax.rem(lax.div(col16, 32), 2) == 0, *found).astype(jnp.bfloat16)
    for dev in ring_line:
        remote(marks.at[z], marks.at[z], marks_send, marks_recv, dev).start()
    begin_on(1, (1, 2))
    send_rows(1, (0, 2))
    begin_on(1, (3,))
    send_rows(1, (3, 1))

    scale = 1.0 / math.sqrt(HEAD_DIM)
    to_log2 = scale * math.log2(math.e)
    lane = lax.broadcasted_iota(jnp.int32, (128, 128), 0)
    key_pos = lax.broadcasted_iota(jnp.int32, (256, SEQ), 1).astype(jnp.float32)
    lse_lane = lax.broadcasted_iota(jnp.int32, (256, 128), 1)
    server_home = [at_y(-away(core, s)) for s in range(SUBS)]

    def pick(base):
        return jnp.where(lane == base, 16.0, jnp.where(lane == base + 1, 1.0, 0.0)).astype(jnp.bfloat16)

    def dot(a, b, dims):
        return lax.dot_general(a, b, (dims, ((), ())), preferred_element_type=jnp.float32)

    row128 = lax.broadcasted_iota(jnp.int32, (128, 16), 0)
    col128 = lax.broadcasted_iota(jnp.int32, (128, 16), 1)
    widen = (lax.div(row128, GROUP) == col128).astype(jnp.float32).astype(jnp.bfloat16)

    def make_bounds(chunk, carry):
        wide = jnp.dot(widen, marks[chunk], preferred_element_type=jnp.float32).astype(jnp.bfloat16)
        for s in range(SUBS):
            for which in range(2):
                for e_lo in range(2):
                    base = e_lo * 64 + s * 32 + z * 4 + which * 2
                    bounds[chunk * SUBS + s, which, e_lo * 128:(e_lo + 1) * 128] = dot(
                        wide, pick(base), ((1,), (0,)))
        return carry

    def one_sequence(n, chunk, s):
        q = got[:, s, n, 0].reshape(256, HEAD_DIM)
        g = got[:, s, n, 1].reshape(256, HEAD_DIM)
        k = kv[chunk, :, pl.ds(s * 128, HALF), :].reshape(SEQ, HEAD_DIM)
        v = kv[chunk, :, pl.ds(s * 128 + HALF, HALF), :].reshape(SEQ, HEAD_DIM)
        last, first = [jnp.concatenate([bounds[chunk * SUBS + s, which]] * 4, axis=1)
                       for which in range(2)]
        visible = jnp.logical_and(key_pos <= last, key_pos >= first)
        scores = jnp.where(visible, dot(q, k, ((1,), (1,))) * to_log2, NEG_FILL)
        top = jnp.max(scores, axis=1, keepdims=True)
        p = jnp.exp2(scores - top)
        total = jnp.sum(p, axis=1, keepdims=True)
        inverse = 1.0 / total
        att = (dot(p.astype(jnp.bfloat16), v, ((1,), (0,))) * inverse).astype(jnp.bfloat16)
        delta = jnp.sum(g.astype(jnp.float32) * att.astype(jnp.float32), axis=1, keepdims=True)
        grad = dot(g, v, ((1,), (1,)))
        ds = (p * (grad - delta)).astype(jnp.bfloat16)
        dq = (dot(ds, k, ((1,), (0,))) * (inverse * scale)).astype(jnp.bfloat16)
        res[:, n * 4 + 2 * s] = att.reshape(SLOTS, GROUP, HEAD_DIM)
        res[:, n * 4 + 2 * s + 1] = dq.reshape(SLOTS, GROUP, HEAD_DIM)
        left_over = (top + jnp.log2(total)) * math.log(2.0)
        kept = lse[...]
        for part in range(3):
            term = left_over.astype(jnp.bfloat16).astype(jnp.float32)
            left_over = left_over - term
            kept = jnp.where(lse_lane == part * 16 + chunk * SUBS + s, term, kept)
        lse[...] = kept

    def give(first_tile, count, s):
        tiles = pl.ds(first_tile + s * count, count)
        dst = out.at[x, server_home[s], tiles]
        for e in (0, 2, 3, 1):
            home_y = at_y(y_step(e, core, s))
            for other in range(2):
                home_core = lax.rem(core + other, 2)
                for x_step in (1, 3, 2, 0):
                    home_ctx = lax.rem(x + x_step, NX) * 2 + home_core
                    src = res.at[(e % 2) * 16 + home_ctx * 2 + e // 2, tiles]
                    if e == 1 and other == 0 and x_step == 0:
                        pltpu.make_async_copy(src, dst, res_recv).start()
                    else:
                        remote(src, dst, res_send, res_recv, (z * NY + home_y, home_ctx)).start()

    def rest_of_rows():
        wait_bytes(got.at[:, :, pl.ds(EARLY, PLACES - EARLY)], row_recv.at[1])

    def before(n):
        if n == 0:
            wait_bytes(got.at[:, :, pl.ds(0, EARLY)], row_recv.at[0])
        elif n == 1:
            pass_on(1, (0,))
        elif n == 2:
            pass_on(1, (1,))
        elif n == 3:
            pass_on(1, (2, 3))
            pass_on(2, (0,))
            rest_of_rows()
        elif n == 4:
            pass_on(2, (1,))
        elif n == 5:
            pass_on(2, (2, 3))
        elif n == 7:
            pass_on(3)

    def serve(n, carry):
        for turn in (0, 1, 2, 3, 4, 5, 7):
            pl.when(n == turn)(functools.partial(before, turn))
        chunk = lax.rem(z + lax.div(n + 1, 2) * (2 * lax.rem(n, 2) - 1) + NZ, NZ)

        for s in range(SUBS):
            one_sequence(n, chunk, s)
            give(n * 4, 2, s)
        return carry

    lse[...] = jnp.zeros_like(lse)
    pass_on(0)
    wait_bytes(marks.at[pl.ds(0, NZ - 1)], marks_recv)
    lax.fori_loop(0, NZ, make_bounds, 0)
    lax.fori_loop(0, PLACES, serve, 0)
    for s in range(SUBS):
        res[:, 4 * PLACES + s] = lse[...].astype(jnp.bfloat16).reshape(SLOTS, GROUP, 128)
    for s in range(SUBS):
        give(4 * PLACES, 1, s)

    sent = pl.ds(0, SLOTS - 1)
    wait_bytes(rows.at[sent, :, pl.ds(0, EARLY)], row_send.at[0])
    wait_bytes(rows.at[sent, :, pl.ds(EARLY, PLACES - EARLY)], row_send.at[1])
    wait_bytes(kv.at[0, pl.ds(0, 4)], kvb_send)
    wait_bytes(marks_in.at[0], markb_send)
    wait_bytes(marks.at[pl.ds(0, NZ - 1)], marks_send)

    @pl.when(core == 0)
    def _():
        wait_bytes(kv.at[0, pl.ds(0, 3)], kva_send)
        wait_bytes(marks_in.at[0, pl.ds(0, 6)], marka_send)

    @pl.when(core != 0)
    def _():
        wait_bytes(kv.at[0, pl.ds(0, 4)], kva_send)
        wait_bytes(marks_in.at[0], marka_send)

    for step in range(4):
        for way in range(2):
            wait_bytes(kv.at[0] if step < 3 else kv.at[0, pl.ds(0, 4)], ring_send.at[way, step])
    wait_bytes(res.at[sent], res_send)
    wait_bytes(out, res_recv)


def order_results(got, attended, lse, grad, held, attended_rows, lse_rows, grad_rows,
                  load, store, lse_store):
    z = lax.div(lax.axis_index("dp"), NY)

    def load_part(n):
        tiles = pl.ds(4 * n, 4) if n < PLACES else pl.ds(4 * PLACES, SUBS)
        return pltpu.make_async_copy(got.at[:, :, tiles], held.at[:, :, tiles], load.at[n])

    def store_part(n, which):
        chunk = lax.rem(z + ((n + 1) // 2) * (2 * (n % 2) - 1) + NZ, NZ)
        lines = pl.ds(pl.multiple_of(chunk * 16, 16), 16)
        source, target = ((attended_rows, attended), (grad_rows, grad))[which]
        return lines, source, pltpu.make_async_copy(source.at[lines], target.at[lines], store.at[which, n])

    order = [PLACES] + list(range(PLACES))
    for n in order:
        load_part(n).start()
    load_part(PLACES).wait()
    column = lax.broadcasted_iota(jnp.int32, (128, 128), 1)
    source = lax.broadcasted_iota(jnp.int32, (128, 128), 0)
    target = lax.div(lax.rem(source, 16), 2) * 16 + lax.rem(source, 2)
    target = jnp.where(source < 48, target, -128)
    total = jnp.zeros((HEADS, 128), jnp.float32)
    for home_y in range(NY):
        terms = [held[:, home_y, 4 * PLACES + s].reshape(HEADS, 128).astype(jnp.float32)
                 for s in range(SUBS)]
        terms = jnp.where(lax.rem(column[:HEADS], 2) == 0, *terms).astype(jnp.bfloat16)
        place = (column == target + home_y * SUBS).astype(jnp.float32).astype(jnp.bfloat16)
        total = total + jnp.dot(terms, place, preferred_element_type=jnp.float32)
    lse_rows[...] = total
    lse_copy = pltpu.make_async_copy(lse_rows, lse, lse_store)
    lse_copy.start()
    for n in range(PLACES):
        load_part(n).wait()
        for which in range(2):
            lines, result, copy = store_part(n, which)
            for head in range(KV_HEADS):
                cols = slice(head * GROUP * HEAD_DIM, (head + 1) * GROUP * HEAD_DIM)
                block = jnp.stack([held[head, :, 4 * n + 2 * s + which] for s in range(SUBS)], axis=1)
                result[lines, cols] = block.reshape(16, GROUP * HEAD_DIM)
            copy.start()
    for n in range(PLACES):
        for which in range(2):
            store_part(n, which)[2].wait()
    lse_copy.wait()


def local(queries, key_rows, value_rows, out_grad, doc_lengths, served_positions):
    bf16 = jnp.bfloat16
    dma = pltpu.SemaphoreType.DMA
    hbm = pl.BlockSpec(memory_space=pltpu.HBM)
    wide = HEADS * HEAD_DIM
    thin = KV_HEADS * HEAD_DIM
    result = pl.pallas_call(
        kernel,
        out_shape=jax.ShapeDtypeStruct((KV_HEADS, NY, TILES, GROUP, HEAD_DIM), bf16),
        in_specs=[hbm] * 6,
        out_specs=hbm,
        scratch_shapes=[
            pltpu.VMEM((NZ * 16, wide), bf16),
            pltpu.VMEM((NZ * 16, wide), bf16),
            pltpu.VMEM((128, thin), bf16),
            pltpu.VMEM((128, thin), bf16),
            pltpu.VMEM((SUBS, 8), jnp.int32),
            pltpu.VMEM((SUBS, HALF), jnp.int32),
            pltpu.VMEM((SLOTS, SUBS, PLACES, 2, GROUP, HEAD_DIM), bf16),
            pltpu.VMEM((KV_HEADS, KV_ROWS, HEAD_DIM), bf16),
            pltpu.VMEM((2, 16, 128), bf16),
            pltpu.VMEM((SUBS, NCTX, 16, 128), bf16),
            pltpu.VMEM((NZ, 16, 128), bf16),
            pltpu.VMEM((NZ * SUBS, 2, SLOTS * GROUP, 128), jnp.float32),
            pltpu.VMEM((NZ, NCTX, KV_ROWS, HEAD_DIM), bf16),
            pltpu.VMEM((SLOTS, SUBS, PLACES, 2, GROUP, HEAD_DIM), bf16),
            pltpu.VMEM((SLOTS, TILES, GROUP, HEAD_DIM), bf16),
            pltpu.VMEM((SLOTS * GROUP, 128), jnp.float32),
            pltpu.SemaphoreType.REGULAR,
            dma((2, NZ)), dma((4,)), dma((2,)), dma((2,)), dma, dma, dma((NX,)),
            dma((2, 4)), dma((2, 4, NX)), dma, dma, dma, dma, dma, dma, dma,
        ],
        compiler_params=pltpu.CompilerParams(
            collective_id=0, has_side_effects=True, vmem_limit_bytes=VMEM_BYTES
        ),
        cost_estimate=pl.CostEstimate(flops=4 * 10**9, bytes_accessed=8 * 2**20,
                                      transcendentals=2 * 2**20),
    )(queries, out_grad, key_rows, value_rows, doc_lengths,
      served_positions.reshape(NZ * NY, SUBS).T)

    attended, lse, grad = pl.pallas_call(
        order_results,
        out_shape=(
            jax.ShapeDtypeStruct((NZ * 16, wide), bf16),
            jax.ShapeDtypeStruct((HEADS, 128), jnp.float32),
            jax.ShapeDtypeStruct((NZ * 16, wide), bf16),
        ),
        in_specs=[hbm],
        out_specs=(hbm, hbm, hbm),
        scratch_shapes=[
            pltpu.VMEM((KV_HEADS, NY, TILES, GROUP, HEAD_DIM), bf16),
            pltpu.VMEM((NZ * 16, wide), bf16),
            pltpu.VMEM((HEADS, 128), jnp.float32),
            pltpu.VMEM((NZ * 16, wide), bf16),
            dma((PLACES + 1,)), dma((2, PLACES)), dma,
        ],
        compiler_params=pltpu.CompilerParams(vmem_limit_bytes=VMEM_BYTES),
        cost_estimate=pl.CostEstimate(flops=0, bytes_accessed=4 * 2**20, transcendentals=0),
    )(result)
    return attended, lse.T, grad


def solution(mesh):
    in_specs = (
        P(("dp", "ctx"), None),
        P(("dp", "ctx"), None),
        P(("dp", "ctx"), None),
        P(("dp", "ctx"), None),
        P("dp", None),
        P("dp", "ctx", None, None),
    )
    out_specs = (P(("dp", "ctx"), None), P(("dp", "ctx"), None), P(("dp", "ctx"), None))
    return jax.shard_map(local, mesh=mesh, in_specs=in_specs, out_specs=out_specs, check_vma=False)
```
